32 devices in a mesh: tile: 4 (over x, core), orient: 8 (over z, y).
Axes of the slice: x: 2, y: 2, z: 4, core: 2. Of those that a mesh axis runs over, the one named last changes fastest.
Arguments:
- micrograph: bfloat16 [1024, 512], P('tile'), may hold values from -140 to 140
- templates: bfloat16 [16, 384, 384], P('orient', 'tile'), may hold values from -6 to 6
- defocus: float32 [4], replicated, may hold values from 8 to 40
- group_of_tile: int32 [4], P('tile'), may hold values from 0 to 3
Outputs:
- top_score: float32 [1024, 128], P(('tile', 'orient'))
- zscore: float32 [1024, 128], P(('tile', 'orient'))
The draws below stay inside these ranges and needn't reach their ends.
All inputs are finite; a program needn't handle non-finite values.
Results may differ from the reference program's by a relative error of at most 0.0085.
Values may be sent and summed in bfloat16 or wider, within the bound.
No kernel may reach another device: no remote copies, remote signals or barrier semaphores. Data moves between devices by JAX's collectives and lax.ppermute only.
A program may use at most 64 MiB of HBM per device.

```python
import math
import jax
import jax.numpy as jnp
from jax import lax

TS = 384
STRIP = 256
OUTC = 128
GROUPS = 4
ROWS = 1024
LROW = 640
LCOL = 512
ORIENTS = 16
N_TILE = 4


def draw_micrograph(key, part):
    row_key, col_key, pixel_key = jax.random.split(key, 3)
    row_count = STRIP * N_TILE
    col_count = OUTC + TS
    position = jnp.arange(row_count, dtype=jnp.float32) / row_count
    row_scale = jnp.exp(jnp.log(3.0) * position + jnp.log(3.0) * jax.random.uniform(row_key, (row_count,), jnp.float32))
    col_scale = jnp.exp(jnp.log(3.0) * jax.random.uniform(col_key, (col_count,), jnp.float32))
    pixels = jnp.clip(jax.random.normal(pixel_key, (row_count, col_count), jnp.float32), -5.0, 5.0)
    return (pixels * row_scale[:, None] * col_scale[None, :]).astype(jnp.bfloat16)


def plant(drawn, rng, smallest, high):
    dims = drawn.shape
    place = [jax.random.randint(jax.random.fold_in(rng, axis), (), 0, dims[axis]) for axis in range(len(dims))]
    drawn = drawn.at[tuple(place)].set(smallest)
    longest = dims.index(max(dims))
    place[longest] = (place[longest] + 1) % dims[longest]
    return drawn.at[tuple(place)].set(high)


def levels(stream_key, extent, pieces, smallest, largest):
    factor_of = 1.0
    for dim, parts in pieces:
        steps = jax.random.uniform(jax.random.fold_in(jax.random.fold_in(stream_key, 6), dim), (parts,), jnp.float32, smallest / len(pieces), largest / len(pieces))
        factor_of = factor_of * jnp.repeat(jnp.exp(steps), extent[dim] // parts).reshape((-1,) + (1,) * (len(extent) - 1 - dim))
    return factor_of


def gaussian(key, extent, spread, most, cuts=(), held_as=jnp.bfloat16):
    entries = spread * jax.random.normal(key, extent, jnp.float32)
    if cuts:
        entries = entries * levels(key, extent, cuts, -0.22, 0.18)
    return jnp.clip(entries, -most, most).astype(held_as)


def setup_inputs(seed: int = 0) -> dict:
    keys = jax.random.split(jax.random.key(seed), 5)
    return {
        "micrograph": draw_micrograph(jax.random.fold_in(keys[4], 71), 0),
        "templates": gaussian(keys[1], (ORIENTS, TS, TS), 1.0, 6.0, ((0, 8), (1, 4))),
        "defocus": jnp.clip(jnp.exp(jax.random.uniform(keys[2], (GROUPS,), jnp.float32, math.log(8.0), math.log(40.0))), 8.0, 40.0),
        "group_of_tile": plant(jax.random.randint(keys[3], (N_TILE,), 0, GROUPS), jax.random.fold_in(keys[3], 1), 0, GROUPS - 1).astype(jnp.int32),
    }


def twiddle(row_count, col_count, modulus, sign_value):
    freq_index = jnp.arange(row_count, dtype=jnp.int32)[:, None]
    place_index = jnp.arange(col_count, dtype=jnp.int32)[None, :]
    residue = freq_index * place_index % modulus
    mirrored = modulus - residue
    lowest = jnp.minimum(residue, mirrored)
    flipped = jnp.where(residue > mirrored, -1.0, 1.0).astype(jnp.float32)
    angle = lowest.astype(jnp.float32) * jnp.float32(2.0 * math.pi / modulus)
    return (jnp.cos(angle).astype(jnp.bfloat16), (sign_value * flipped * jnp.sin(angle)).astype(jnp.bfloat16))

def quarter_turn(stacked):
    middle = stacked.shape[-1] // 2
    return jnp.concatenate([-stacked[..., middle:], stacked[..., :middle]], axis=-1)

def rotate_apply(table_cos, table_sin, stacked):
    return jnp.dot(table_cos, stacked, preferred_element_type=jnp.float32) + jnp.dot(table_sin, quarter_turn(stacked), preferred_element_type=jnp.float32)

def signed_freq(length):
    index = jnp.arange(length, dtype=jnp.int32)
    return jnp.where(2 * index < length, index, index - length).astype(jnp.float32) / length

def ctf_table(defocus_value):
    row_freq = signed_freq(LROW)
    col_freq = signed_freq(LCOL)
    radius = row_freq[:, None] ** 2 + col_freq[None, :] ** 2
    return -jnp.sin(jnp.float32(math.pi) * defocus_value * radius + 0.07)

def reference(micrograph, templates, defocus, group_of_tile):
    col_cos, col_sin = twiddle(LCOL, LCOL, LCOL, -1.0)
    col_table = jnp.concatenate([col_cos, col_sin], axis=1)
    row_cos, row_sin = twiddle(LROW, LROW, LROW, -1.0)
    back_cos, back_sin = twiddle(LCOL, OUTC, LCOL, 1.0)
    back_table = jnp.concatenate([jnp.concatenate([back_cos, back_sin], 1), jnp.concatenate([-back_sin, back_cos], 1)], 0)
    out_cos, out_sin = twiddle(STRIP, LROW, LROW, 1.0)
    padded = jnp.concatenate([micrograph, jnp.zeros((2 * STRIP, LCOL), jnp.bfloat16)], 0)

    def spectrum(tile_index):
        window = lax.dynamic_slice_in_dim(padded, tile_index * STRIP, LROW, 0)
        column_part = jnp.dot(window, col_table, preferred_element_type=jnp.float32).astype(jnp.bfloat16)
        return rotate_apply(row_cos, row_sin, column_part)
    spectra = lax.map(spectrum, jnp.arange(N_TILE, dtype=jnp.int32))
    power_map = lax.optimization_barrier(jnp.sum(spectra[..., :LCOL] ** 2 + spectra[..., LCOL:] ** 2, axis=0)) / N_TILE
    whiten = lax.rsqrt(power_map + jnp.mean(power_map))
    whiten_both = jnp.concatenate([whiten, whiten], axis=1)
    widened = templates.astype(jnp.float32)
    tpl_spec = jnp.einsum('abc,cd->abd', widened, col_table[:TS].astype(jnp.float32)).astype(jnp.bfloat16)
    sums = lax.optimization_barrier(jnp.sum(widened, axis=(1, 2)))
    squares = lax.optimization_barrier(jnp.sum(widened * widened, axis=(1, 2)))
    mean_tpl = sums / (TS * TS)
    spread_tpl = jnp.sqrt(squares / (TS * TS) - mean_tpl * mean_tpl + 1e-05)
    raw_spec = lax.map(lambda single: rotate_apply(row_cos[:, :TS], row_sin[:, :TS], single), tpl_spec)
    row_sum_cos = lax.optimization_barrier(jnp.sum(row_cos[:, :TS].astype(jnp.float32), axis=1))
    row_sum_sin = lax.optimization_barrier(jnp.sum(row_sin[:, :TS].astype(jnp.float32), axis=1))
    col_sums = lax.optimization_barrier(jnp.sum(col_table[:TS].astype(jnp.float32), axis=0))
    col_sum_cos = col_sums[:LCOL]
    col_sum_sin = col_sums[LCOL:]
    box = jnp.concatenate([row_sum_cos[:, None] * col_sum_cos[None, :] - row_sum_sin[:, None] * col_sum_sin[None, :], row_sum_cos[:, None] * col_sum_sin[None, :] + row_sum_sin[:, None] * col_sum_cos[None, :]], axis=1)

    def per_tile(tile_index):
        weighted = spectra[tile_index] * whiten_both
        ctf_map = ctf_table(defocus[group_of_tile[tile_index]])
        image_re = weighted[:, :LCOL]
        image_im = weighted[:, LCOL:]

        def per_template(running, inputs):
            raw_single, mean_single, spread_single = inputs
            shaped = (raw_single - mean_single * box) / spread_single
            shape_re = shaped[:, :LCOL]
            shape_im = shaped[:, LCOL:]
            product = jnp.concatenate([(image_re * shape_re + image_im * shape_im) * ctf_map, (image_im * shape_re - image_re * shape_im) * ctf_map], axis=1).astype(jnp.bfloat16)
            partial_back = jnp.dot(product, back_table, preferred_element_type=jnp.float32).astype(jnp.bfloat16)
            score = (jnp.dot(out_cos, partial_back[:, :OUTC], preferred_element_type=jnp.float32) - jnp.dot(out_sin, partial_back[:, OUTC:], preferred_element_type=jnp.float32)) / (LROW * LCOL)
            best, score_sum, score_squares = running
            return ((jnp.maximum(best, score), score_sum + score, score_squares + score * score), None)
        start_state = (jnp.full((STRIP, OUTC), -jnp.inf, jnp.float32), jnp.zeros((STRIP, OUTC), jnp.float32), jnp.zeros((STRIP, OUTC), jnp.float32))
        final_state, _ = lax.scan(per_template, start_state, (raw_spec, mean_tpl, spread_tpl))
        return final_state
    best, score_sum, score_squares = lax.map(per_tile, jnp.arange(N_TILE, dtype=jnp.int32))
    best = best.reshape(ROWS, OUTC)
    score_mean = score_sum.reshape(ROWS, OUTC) / ORIENTS
    score_var = score_squares.reshape(ROWS, OUTC) / ORIENTS - score_mean * score_mean
    return (best, (best - score_mean) / jnp.sqrt(score_var + 1e-05))
```

```python
import functools
import math

import jax
import jax.numpy as jnp
import ml_dtypes
import numpy as np
from jax import lax
from jax.experimental import pallas as pl
from jax.experimental.pallas import tpu as pltpu
from jax.sharding import PartitionSpec as P

TS = 384
STRIP = 256
OUTC = 128
CHUNK = 16
VMEM_BYTES = 40 * 1024 * 1024


def cos_sin(freqs, places, modulus):
    residue = freqs[:, None] * places[None, :] % modulus
    lowest = np.minimum(residue, modulus - residue)
    flipped = np.where(residue > modulus - residue, -1.0, 1.0).astype(np.float32)
    angle = lowest.astype(np.float32) * np.float32(2.0 * math.pi / modulus)
    sine = np.where(2 * lowest == modulus, np.float32(0.0), flipped * np.sin(angle))
    return np.cos(angle).astype(np.float32), sine.astype(np.float32)


def round_up(value, multiple):
    return -(-value // multiple) * multiple


@functools.lru_cache(maxsize=None)
def tables(width_rows, width_cols):
    half = width_cols // 2
    rows = width_rows // 2 + 1
    padded = round_up(rows, CHUNK)
    bf16 = ml_dtypes.bfloat16
    places = np.arange(width_cols)
    cos_v, sin_v = cos_sin(np.arange(half + 1), places, width_cols)
    packed_sin = sin_v[:half].copy()
    forward_sin = -packed_sin
    forward_sin[0] = cos_v[half]
    packed_sin[0] = cos_v[half]
    col = np.concatenate([cos_v[:half], forward_sin], 0).T.astype(bf16)
    back = (2.0 * np.concatenate([cos_v[:half], packed_sin], 0)[:, :OUTC].astype(bf16).astype(np.float32)).astype(bf16)
    cos_u, sin_u = cos_sin(np.arange(rows), np.arange(width_rows), width_rows)
    row = np.zeros((2 * padded, width_rows), np.float32)
    row[:rows] = cos_u
    row[padded : padded + rows] = -sin_u
    row = row.astype(bf16)
    weight = np.ones((rows, 1), np.float32)
    weight[0] = weight[-1] = 0.5
    out = np.zeros((2 * padded, STRIP), np.float32)
    out[:rows] = cos_u[:, :STRIP].astype(bf16).astype(np.float32) * weight
    out[padded : padded + rows] = sin_u[:, :STRIP].astype(bf16).astype(np.float32) * weight
    out = np.ascontiguousarray(out.T).astype(bf16)
    row_sum = row[:, :TS].astype(np.float32).sum(1, keepdims=True)
    col_sum = col[:TS].astype(np.float32).sum(0, keepdims=True)
    u = np.minimum(np.arange(padded), rows - 1).astype(np.float32) / np.float32(width_rows)
    v = np.arange(half).astype(np.float32) / np.float32(width_cols)
    v_last = v.copy()
    v_last[0] = 0.5
    radius = np.stack([u[:, None] ** 2 + w[None, :] ** 2 for w in (v, v_last)])
    return col, row, back, out, row_sum.astype(np.float32), col_sum.astype(np.float32), radius


def gather_blocks(value, axis):
    count = lax.axis_size(axis)
    place = lax.axis_index(axis)
    if count & (count - 1):
        whole = lax.all_gather(value, axis, axis=0)
        return [whole[j] for j in range(count)], jnp.arange(count, dtype=jnp.int32)
    held, index = [value], [0]
    step = count // 2
    while step:
        pairs = [(source, source ^ step) for source in range(count)]
        held = held + [lax.ppermute(block, axis, pairs) for block in held]
        index = index + [j ^ step for j in index]
        step //= 2
    return held, jnp.stack([place ^ j for j in index]).astype(jnp.int32)


def first_column(shape):
    return lax.broadcasted_iota(jnp.int32, shape, 1) == 0


def both_signs(cc, cs, sc, ss, first):
    plus_re = cc - jnp.where(first, 0.0, ss)
    plus_im = jnp.where(first, 0.0, cs) + sc
    minus_re = jnp.where(first, cs, cc + ss)
    minus_im = jnp.where(first, ss, cs - sc)
    return plus_re, plus_im, minus_re, minus_im


def spectrum_kernel(count, place_ref, *refs):
    blocks = refs[:count]
    col_ref, row_ref, ctf_ref, weighted_ref, part_ref, quad_ref, own_ref, power_ref = refs[count:]
    padded = row_ref.shape[0] // 2
    width_rows = row_ref.shape[1]
    half = col_ref.shape[1] // 2
    width_cols = col_ref.shape[0]
    first = first_column((CHUNK, half))
    part_ref[count * STRIP :, :] = jnp.zeros((part_ref.shape[0] - count * STRIP, 2 * half), jnp.bfloat16)
    for j in range(count):
        start = pl.multiple_of(place_ref[j] * STRIP, STRIP)
        part_ref[pl.ds(start, STRIP), :] = jnp.dot(
            blocks[j][...], col_ref[...], preferred_element_type=jnp.float32
        ).astype(jnp.bfloat16)
    for j in range(count):
        start = pl.multiple_of(place_ref[j] * STRIP, STRIP)
        quad_ref[...] = jnp.dot(
            row_ref[...], part_ref[pl.ds(start, width_rows), :], preferred_element_type=jnp.float32
        )
        for r in range(0, padded, CHUNK):
            up, down = slice(r, r + CHUNK), slice(padded + r, padded + r + CHUNK)
            signs = both_signs(
                quad_ref[up, :half], quad_ref[up, half:], quad_ref[down, :half], quad_ref[down, half:], first
            )
            plus = signs[0] * signs[0] + signs[1] * signs[1]
            minus = signs[2] * signs[2] + signs[3] * signs[3]
            if j == 0:
                for k in range(4):
                    own_ref[k, up] = signs[k]
                power_ref[0, up] = plus
                power_ref[1, up] = minus
            else:
                power_ref[0, up] += plus
                power_ref[1, up] += minus
    total = jnp.zeros((CHUNK, half), jnp.float32)
    for r in range(0, padded, CHUNK):
        total = total + (power_ref[0, r : r + CHUNK] + power_ref[1, r : r + CHUNK])
    last = width_rows // 2
    ends = (power_ref[0, 0:1] + power_ref[1, 0:1]) + (power_ref[0, last : last + 1] + power_ref[1, last : last + 1])
    mean = (2.0 * jnp.sum(total, keepdims=True) - jnp.sum(ends, keepdims=True)) / (count * width_rows * width_cols)
    for r in range(0, padded, CHUNK):
        up = slice(r, r + CHUNK)
        for side in range(2):
            gain = lax.rsqrt(power_ref[side, up] * (1.0 / count) + mean) * ctf_ref[side, up]
            weighted_ref[2 * side, up] = own_ref[2 * side, up] * gain
            weighted_ref[2 * side + 1, up] = own_ref[2 * side + 1, up] * gain


def score_kernel(count, place_ref, *refs):
    blocks = refs[:count]
    (weighted_ref, col_ref, row_ref, back_ref, out_ref, row_sum_ref, col_sum_ref) = refs[count : count + 7]
    score_ref, whole_ref, quad_ref, product_ref = refs[count + 7 :]
    padded = row_ref.shape[0] // 2
    half = col_ref.shape[1] // 2
    scale = 1.0 / (row_ref.shape[1] * col_ref.shape[0])
    first = first_column((CHUNK, half))
    tpl_count, depth = blocks[0].shape[:2]
    pieces = score_ref.shape[0]
    for index in range(tpl_count):
        sums = jnp.zeros((1, 1), jnp.float32)
        squares = jnp.zeros((1, 1), jnp.float32)
        for j in range(count):
            block = blocks[j][index]
            wide = block.astype(jnp.float32)
            sums = sums + jnp.sum(wide, keepdims=True)
            squares = squares + jnp.sum(wide * wide, keepdims=True)
            start = pl.multiple_of(place_ref[j] * depth, depth)
            whole_ref[index, pl.ds(start, depth), :] = block.astype(whole_ref.dtype)
        mean = sums / (TS * TS)
        spread = jnp.sqrt(squares / (TS * TS) - mean * mean + 1e-05)
        partial = jnp.dot(
            whole_ref[index].astype(jnp.bfloat16), col_ref[:TS, :], preferred_element_type=jnp.float32
        ).astype(jnp.bfloat16)
        quad_ref[...] = jnp.dot(row_ref[:, :TS], partial, preferred_element_type=jnp.float32)
        col_sum = mean * col_sum_ref[...]
        for r in range(0, padded, CHUNK):
            up, down = slice(r, r + CHUNK), slice(padded + r, padded + r + CHUNK)
            upper = quad_ref[up, :] - row_sum_ref[up, :] * col_sum
            lower = quad_ref[down, :] - row_sum_ref[down, :] * col_sum
            a, b, c, d = both_signs(upper[:, :half], upper[:, half:], lower[:, :half], lower[:, half:], first)
            p, q, s, t = (weighted_ref[k, up] for k in range(4))
            plus_re = p * a + q * b
            plus_im = q * a - p * b
            minus_re = s * c + t * d
            minus_im = t * c - s * d
            product_ref[up, :half] = (plus_re + jnp.where(first, 0.0, minus_re)).astype(jnp.bfloat16)
            product_ref[up, half:] = jnp.where(first, minus_re, -(plus_im + minus_im)).astype(jnp.bfloat16)
            product_ref[down, :half] = (jnp.where(first, 0.0, minus_im) - plus_im).astype(jnp.bfloat16)
            product_ref[down, half:] = jnp.where(first, -minus_im, minus_re - plus_re).astype(jnp.bfloat16)
        back = jnp.dot(product_ref[...], back_ref[...], preferred_element_type=jnp.float32).astype(jnp.bfloat16)
        score = jnp.dot(out_ref[...], back, preferred_element_type=jnp.float32) * (scale / spread)
        score_ref[:, index] = score.reshape(pieces, STRIP // pieces, OUTC).astype(jnp.bfloat16)


def on_device(kernel, operands, scratch, result):
    vmem, smem = pl.BlockSpec(memory_space=pltpu.VMEM), pl.BlockSpec(memory_space=pltpu.SMEM)
    return pl.pallas_call(
        kernel,
        out_shape=result,
        in_specs=[smem] + [vmem] * (len(operands) - 1),
        out_specs=vmem,
        scratch_shapes=scratch,
        compiler_params=pltpu.CompilerParams(vmem_limit_bytes=VMEM_BYTES),
    )(*operands)


def local(micrograph, templates, defocus, group_of_tile):
    width_cols = micrograph.shape[1]
    width_rows = STRIP + TS
    tpl_count, depth = templates.shape[:2]
    count = lax.axis_size("tile")
    orient_count = lax.axis_size("orient")
    col, row, back, out, row_sum, col_sum, radius = tables(width_rows, width_cols)
    padded, half = row.shape[0] // 2, width_cols // 2
    strips, places = gather_blocks(micrograph, "tile")
    pieces, _ = gather_blocks(templates, "tile")
    ctf = -jnp.sin(jnp.float32(math.pi) * defocus[group_of_tile[0]] * radius + 0.07)
    plane = (padded, half)
    weighted = on_device(
        functools.partial(spectrum_kernel, count),
        [places, *strips, col, row, ctf],
        [
            pltpu.VMEM((count * STRIP + TS, width_cols), jnp.bfloat16),
            pltpu.VMEM((2 * padded, width_cols), jnp.float32),
            pltpu.VMEM((4, *plane), jnp.float32),
            pltpu.VMEM((2, *plane), jnp.float32),
        ],
        jax.ShapeDtypeStruct((4, *plane), jnp.float32),
    )
    scores = on_device(
        functools.partial(score_kernel, count),
        [places, *pieces, weighted, col, row, back, out, row_sum, col_sum],
        [
            pltpu.VMEM((tpl_count, TS, TS), jnp.bfloat16 if depth % 16 == 0 else jnp.float32),
            pltpu.VMEM((2 * padded, width_cols), jnp.float32),
            pltpu.VMEM((2 * padded, width_cols), jnp.bfloat16),
        ],
        jax.ShapeDtypeStruct((orient_count, tpl_count, STRIP // orient_count, OUTC), jnp.bfloat16),
    )
    received = lax.all_to_all(scores, "orient", split_axis=0, concat_axis=0, tiled=True).astype(jnp.float32)
    orient_total = tpl_count * orient_count
    best = jnp.max(received, axis=(0, 1))
    score_mean = jnp.sum(received, axis=(0, 1)) / orient_total
    score_var = jnp.sum(received * received, axis=(0, 1)) / orient_total - score_mean * score_mean
    return (best, (best - score_mean) / jnp.sqrt(score_var + 1e-05))


def solution(mesh):
    placed = (P("tile", None), P("orient", "tile", None), P(), P("tile"))
    return jax.shard_map(
        local,
        mesh=mesh,
        in_specs=placed,
        out_specs=(P(("tile", "orient"), None), P(("tile", "orient"), None)),
        check_vma=False,
    )
```

```python
import functools
import math

import jax
import jax.numpy as jnp
import ml_dtypes
import numpy as np
from jax import lax
from jax.experimental import pallas as pl
from jax.experimental.pallas import tpu as pltpu
from jax.sharding import PartitionSpec as P

TS = 384
STRIP = 256
OUTC = 128
CHUNK = 16
VMEM_BYTES = 40 * 1024 * 1024


def cos_sin(freqs, places, modulus):
    residue = freqs[:, None] * places[None, :] % modulus
    lowest = np.minimum(residue, modulus - residue)
    flipped = np.where(residue > modulus - residue, -1.0, 1.0).astype(np.float32)
    angle = lowest.astype(np.float32) * np.float32(2.0 * math.pi / modulus)
    sine = np.where(2 * lowest == modulus, np.float32(0.0), flipped * np.sin(angle))
    return np.cos(angle).astype(np.float32), sine.astype(np.float32)


def round_up(value, multiple):
    return -(-value // multiple) * multiple


@functools.lru_cache(maxsize=None)
def tables(width_rows, width_cols):
    half = width_cols // 2
    rows = width_rows // 2 + 1
    padded = round_up(rows, CHUNK)
    bf16 = ml_dtypes.bfloat16
    places = np.arange(width_cols)
    cos_v, sin_v = cos_sin(np.arange(half + 1), places, width_cols)
    packed_sin = sin_v[:half].copy()
    forward_sin = -packed_sin
    forward_sin[0] = cos_v[half]
    packed_sin[0] = cos_v[half]
    col = np.concatenate([cos_v[:half], forward_sin], 0).T.astype(bf16)
    back = (2.0 * np.concatenate([cos_v[:half], packed_sin], 0)[:, :OUTC].astype(bf16).astype(np.float32)).astype(bf16)
    cos_u, sin_u = cos_sin(np.arange(rows), np.arange(width_rows), width_rows)
    row = np.zeros((2 * padded, width_rows), np.float32)
    row[:rows] = cos_u
    row[padded : padded + rows] = -sin_u
    row = row.astype(bf16)
    weight = np.ones((rows, 1), np.float32)
    weight[0] = weight[-1] = 0.5
    out = np.zeros((2 * padded, STRIP), np.float32)
    out[:rows] = cos_u[:, :STRIP].astype(bf16).astype(np.float32) * weight
    out[padded : padded + rows] = sin_u[:, :STRIP].astype(bf16).astype(np.float32) * weight
    out = np.ascontiguousarray(out.T).astype(bf16)
    row_sum = row[:, :TS].astype(np.float32).sum(1, keepdims=True)
    col_sum = col[:TS].astype(np.float32).sum(0, keepdims=True)
    return col, row, back, out, row_sum, col_sum


def swapped(value, axis, step):
    count = lax.axis_size(axis)
    return lax.ppermute(value, axis, [(source, source ^ step) for source in range(count)])


def spread_out(value, axis):
    held, step = {0: value}, lax.axis_size(axis) // 2
    while step > 1:
        held |= {index ^ step: swapped(block, axis, step) for index, block in held.items()}
        step //= 2
    return [held[index] for index in sorted(held)[1:]]


def first_column(shape):
    return lax.broadcasted_iota(jnp.int32, shape, 1) == 0


def both_signs(cc, cs, sc, ss, first):
    plus_re = cc - jnp.where(first, 0.0, ss)
    plus_im = jnp.where(first, 0.0, cs) + sc
    minus_re = jnp.where(first, cs, cc + ss)
    minus_im = jnp.where(first, ss, cs - sc)
    return plus_re, plus_im, minus_re, minus_im


def quadrants(load, r, padded, half, first):
    up, down = load(slice(r, r + CHUNK)), load(slice(padded + r, padded + r + CHUNK))
    return both_signs(up[:, :half], up[:, half:], down[:, :half], down[:, half:], first)


def dot(left, right):
    return jnp.dot(left, right, preferred_element_type=jnp.float32)


def moments(block):
    wide = block.astype(jnp.float32)
    return jnp.sum(wide, axis=0, keepdims=True), jnp.sum(wide * wide, axis=0, keepdims=True)


def early_kernel(
    tile_ref, ctf_ref, strip_b, tpl_b, strip_hbm, tpl_hbm, col_hbm, row_hbm, deep_hbm,
    column_ref, partial_ref, raw_ref, shape_ref, moment_ref,
    strip_a, tpl_a, col_ref, row_ref, deep_ref, order_ref, sems,
):
    tile = tile_ref[0]
    bit, pair = tile & 1, tile >> 1
    padded, half = row_ref.shape[0] // 2, col_ref.shape[1] // 2
    pending = {}

    def fetch(name, source, target, pieces):
        step = target.shape[0] // pieces
        pending[name] = []
        for k in range(pieces):
            number = sum(map(len, pending.values()))
            rows = pl.ds(k * step, step)
            copy = pltpu.make_async_copy(source.at[rows], target.at[rows], sems.at[number])
            copy.start()
            pending[name].append(copy)

    def ready(name):
        for copy in pending[name]:
            copy.wait()

    fetch("strip", strip_hbm, strip_a, 1)
    fetch("col", col_hbm, col_ref, 2)
    fetch("row", row_hbm, row_ref, 3)
    fetch("tpl", tpl_hbm, tpl_a, 1)
    pending["deep"] = [pltpu.make_async_copy(deep_hbm.at[pair], deep_ref, sems.at[7])]
    pending["deep"][0].start()

    ready("strip")
    ready("col")
    for j, strip in enumerate((strip_a, strip_b)):
        start = pl.multiple_of((bit ^ j) * STRIP, STRIP)
        column_ref[pl.ds(start, STRIP), :] = dot(strip[...], col_ref[...]).astype(jnp.bfloat16)
    ready("row")
    partial_ref[0] = dot(row_ref[:, : 2 * STRIP], column_ref[...])
    partial_ref[1] = dot(row_ref[:, :STRIP], column_ref[STRIP:, :])
    ready("tpl")
    mine, depth = raw_ref.shape[0], tpl_a.shape[1]
    for index in range(mine):
        for j, block in enumerate((tpl_a, tpl_b)):
            start = pl.multiple_of((bit ^ j) * depth, depth)
            order_ref[index, pl.ds(start, depth), :] = block[bit * mine + index].astype(order_ref.dtype)
    raw_ref[...] = order_ref[...].astype(jnp.bfloat16)
    ready("deep")
    for index in range(mine):
        for k, moment in enumerate(moments(raw_ref[index])):
            moment_ref[2 * index + k : 2 * index + k + 1, :] = moment
        shape_ref[index] = dot(deep_ref[...], dot(raw_ref[index], col_ref[:TS, :]).astype(jnp.bfloat16))


def ctf_kernel(half, width_rows, tile_ref, group_a, group_b, defocus_ref, ctf_ref):
    bit = tile_ref[0] & 1
    padded = ctf_ref.shape[2]
    u = lax.broadcasted_iota(jnp.int32, (8, round_up(padded, 128)), 1).astype(jnp.float32) / width_rows
    column = lax.broadcasted_iota(jnp.int32, (8, half), 1)
    wrapped = (lax.broadcasted_iota(jnp.int32, (8, half), 0) == 1) & (column == 0)
    v = jnp.where(wrapped, half, column).astype(jnp.float32) / (2 * half)
    for k in range(2):
        turn = jnp.float32(math.pi) * defocus_ref[jnp.where(bit == k, group_a[0], group_b[0])]
        phase_u, phase_v = turn * (u * u) + 0.07, turn * (v * v)
        sin_u, cos_u = jnp.sin(phase_u).T[:padded, :1], jnp.cos(phase_u).T[:padded, :1]
        sin_v, cos_v = jnp.sin(phase_v), jnp.cos(phase_v)
        for side in range(2):
            for r in range(0, padded, CHUNK):
                up = slice(r, r + CHUNK)
                ctf_ref[k, side, up] = -(
                    sin_u[up] * cos_v[side : side + 1] + cos_u[up] * sin_v[side : side + 1]
                )


def spectrum_kernel(count, tile_ref, *refs):
    others = refs[: count - 2]
    (column_ref, partial_ref, ctf_ref, col_ref, row_ref, weighted_ref) = refs[count - 2 : count + 4]
    part_ref, cross_ref, work_ref, power_ref = refs[count + 4 :]
    padded, half = row_ref.shape[0] // 2, col_ref.shape[1] // 2
    width_rows, width_cols = row_ref.shape[1], col_ref.shape[0]
    tile = tile_ref[0]
    bit = tile & 1
    pairs = count // 2
    first = first_column((CHUNK, half))

    def rows_of(pair, offset, length):
        return pl.ds(pl.multiple_of(pair * (2 * STRIP), 2 * STRIP) + offset, length)

    for j in range(2, count):
        start = pl.multiple_of((tile ^ j) * STRIP, STRIP)
        part_ref[pl.ds(start, STRIP), :] = dot(others[j - 2][...], col_ref[...]).astype(jnp.bfloat16)
    if pairs > 1:
        part_ref[rows_of(tile >> 1, 0, 2 * STRIP), :] = column_ref[...]

    def add_power(loads, fresh):
        for r in range(0, padded, CHUNK):
            up = slice(r, r + CHUNK)
            plus, minus = 0.0, 0.0
            for load in loads:
                signs = quadrants(load, r, padded, half, first)
                plus = plus + (signs[0] * signs[0] + signs[1] * signs[1])
                minus = minus + (signs[2] * signs[2] + signs[3] * signs[3])
            power_ref[0, up] = plus if fresh else power_ref[0, up] + plus
            power_ref[1, up] = minus if fresh else power_ref[1, up] + minus

    own = tile >> 1

    @pl.when(own + 1 < pairs)
    def _():
        cross_ref[0] = dot(row_ref[:, 2 * STRIP :], part_ref[rows_of(own + 1, 0, width_rows - 2 * STRIP), :])
        cross_ref[1] = dot(row_ref[:, STRIP:], part_ref[rows_of(own + 1, 0, width_rows - STRIP), :])
        add_power([lambda s, k=k: partial_ref[k, s] + cross_ref[k, s] for k in range(2)], True)

    @pl.when(own + 1 == pairs)
    def _():
        add_power([lambda s, k=k: partial_ref[k, s] for k in range(2)], True)

    for j in range(1, pairs):
        pair = own ^ j

        @pl.when(pair + 1 < pairs)
        def _():
            work_ref[0] = dot(row_ref[...], part_ref[rows_of(pair, 0, width_rows), :])
            work_ref[1] = dot(row_ref[...], part_ref[rows_of(pair, STRIP, width_rows), :])

        @pl.when(pair + 1 == pairs)
        def _():
            work_ref[0] = dot(row_ref[:, : 2 * STRIP], part_ref[rows_of(pair, 0, 2 * STRIP), :])
            work_ref[1] = dot(row_ref[:, :STRIP], part_ref[rows_of(pair, STRIP, STRIP), :])

        add_power([lambda s, k=k: work_ref[k, s] for k in range(2)], False)

    total = jnp.zeros((CHUNK, half), jnp.float32)
    for r in range(0, padded, CHUNK):
        total = total + (power_ref[0, r : r + CHUNK] + power_ref[1, r : r + CHUNK])
    last = width_rows // 2
    ends = (power_ref[0, 0:1] + power_ref[1, 0:1]) + (power_ref[0, last : last + 1] + power_ref[1, last : last + 1])
    mean = (2.0 * jnp.sum(total, keepdims=True) - jnp.sum(ends, keepdims=True)) / (count * width_rows * width_cols)

    def weigh(loads):
        for r in range(0, padded, CHUNK):
            up = slice(r, r + CHUNK)
            gains = [lax.rsqrt(power_ref[side, up] * (1.0 / count) + mean) for side in range(2)]
            for k, load in enumerate(loads):
                signs = quadrants(load, r, padded, half, first)
                for side in range(2):
                    gain = gains[side] * ctf_ref[k, side, up]
                    weighted_ref[k, 2 * side, up] = signs[2 * side] * gain
                    weighted_ref[k, 2 * side + 1, up] = signs[2 * side + 1] * gain

    @pl.when(own + 1 < pairs)
    def _():
        weigh([lambda s, k=k: partial_ref[k, s] + cross_ref[k, s] for k in range(2)])

    @pl.when(own + 1 == pairs)
    def _():
        weigh([lambda s, k=k: partial_ref[k, s] for k in range(2)])


def score_kernel(count, tile_ref, *refs):
    pairs = count // 2
    others = refs[: pairs - 1]
    (weighted_ref, shape_ref, moment_ref, col_ref, deep_ref, back_ref, out_ref, row_sum_ref, col_sum_ref) = refs[
        pairs - 1 : pairs + 8
    ]
    score_ref, quad_ref, product_ref = refs[pairs + 8 :]
    padded, half = deep_ref.shape[1] // 2, col_ref.shape[1] // 2
    scale = 1.0 / ((STRIP + TS) * col_ref.shape[0])
    first = first_column((CHUNK, half))
    pieces, mine = score_ref.shape[:2]
    own = tile_ref[0] >> 1
    for index in range(mine):
        sums, squares = (moment_ref[2 * index + k : 2 * index + k + 1, :] for k in range(2))
        for j in range(1, pairs):
            raw = others[j - 1][index]
            late = dot(deep_ref[own ^ j], dot(raw, col_ref[:TS, :]).astype(jnp.bfloat16))
            quad_ref[...] = late if j == 1 else quad_ref[...] + late
            more = moments(raw)
            sums, squares = sums + more[0], squares + more[1]
        mean = jnp.sum(sums, keepdims=True) / (TS * TS)
        spread = jnp.sqrt(jnp.sum(squares, keepdims=True) / (TS * TS) - mean * mean + 1e-05)
        col_sum = mean * col_sum_ref[...]

        def load(s):
            known = shape_ref[index, s] + quad_ref[s] if pairs > 1 else shape_ref[index, s]
            return known - row_sum_ref[s, :] * col_sum

        for r in range(0, padded, CHUNK):
            up, down = slice(r, r + CHUNK), slice(padded + r, padded + r + CHUNK)
            a, b, c, d = quadrants(load, r, padded, half, first)
            for k in range(2):
                p, q, s, t = (weighted_ref[k, m, up] for m in range(4))
                plus_re = p * a + q * b
                plus_im = q * a - p * b
                minus_re = s * c + t * d
                minus_im = t * c - s * d
                product_ref[k, up, :half] = (plus_re + jnp.where(first, 0.0, minus_re)).astype(jnp.bfloat16)
                product_ref[k, up, half:] = jnp.where(first, minus_re, -(plus_im + minus_im)).astype(jnp.bfloat16)
                product_ref[k, down, :half] = (jnp.where(first, 0.0, minus_im) - plus_im).astype(jnp.bfloat16)
                product_ref[k, down, half:] = jnp.where(first, -minus_im, minus_re - plus_re).astype(jnp.bfloat16)
        for k in range(2):
            back = dot(product_ref[k], back_ref[...]).astype(jnp.bfloat16)
            score = (dot(out_ref[...], back) * (scale / spread)).reshape(pieces // 2, 2 * STRIP // pieces, OUTC)
            score_ref[k * (pieces // 2) : (k + 1) * (pieces // 2), index] = score.astype(jnp.bfloat16)


def on_device(kernel, scalars, operands, tables_in_hbm, scratch, result, flops):
    vmem, smem, hbm = (pl.BlockSpec(memory_space=space) for space in (pltpu.VMEM, pltpu.SMEM, pltpu.HBM))
    return pl.pallas_call(
        kernel,
        out_shape=result,
        in_specs=[smem] * len(scalars) + [vmem] * len(operands) + [hbm] * len(tables_in_hbm),
        out_specs=jax.tree.map(lambda _: vmem, result),
        scratch_shapes=scratch,
        compiler_params=pltpu.CompilerParams(vmem_limit_bytes=VMEM_BYTES),
        cost_estimate=pl.CostEstimate(flops=flops, bytes_accessed=0, transcendentals=0),
    )(*scalars, *operands, *tables_in_hbm)


def local(micrograph, templates, defocus, group_of_tile):
    width_cols = micrograph.shape[1]
    width_rows = STRIP + TS
    tpl_count, depth = templates.shape[:2]
    count = lax.axis_size("tile")
    orient_count = lax.axis_size("orient")
    col, row, back, out, row_sum, col_sum = tables(width_rows, width_cols)
    deep = np.stack(np.split(row[:, :TS], count // 2, axis=1))
    padded, half = row.shape[0] // 2, width_cols // 2
    tile = lax.axis_index("tile").astype(jnp.int32).reshape(1)
    plane, quads = (padded, half), (2 * padded, width_cols)
    f32, bf16 = jnp.float32, jnp.bfloat16
    mine = tpl_count // 2
    pass_flops = 2 * quads[0] * quads[1] * STRIP

    strips = spread_out(micrograph, "tile")
    held = [micrograph, templates, col, row, deep]
    ctf = on_device(
        functools.partial(ctf_kernel, half, width_rows),
        [tile, group_of_tile, swapped(group_of_tile, "tile", 1), defocus],
        [],
        [],
        [],
        jax.ShapeDtypeStruct((2, 2, *plane), f32),
        24 * pass_flops,
    )
    early = on_device(
        early_kernel,
        [tile],
        [ctf, swapped(micrograph, "tile", 1), swapped(templates, "tile", 1)],
        held,
        [pltpu.VMEM(a.shape if a is not deep else a.shape[1:], a.dtype) for a in held]
        + [
            pltpu.VMEM((mine, 2 * depth, TS), bf16 if depth % 16 == 0 else f32),
            pltpu.SemaphoreType.DMA((10,)),
        ],
        (
            jax.ShapeDtypeStruct((2 * STRIP, width_cols), bf16),
            jax.ShapeDtypeStruct((2, *quads), f32),
            jax.ShapeDtypeStruct((mine, 2 * depth, TS), bf16),
            jax.ShapeDtypeStruct((mine, *quads), f32),
            jax.ShapeDtypeStruct((round_up(2 * mine, 8), TS), f32),
        ),
        12 * pass_flops,
    )
    column, partial, raw, shape, moment = early
    strips, column = lax.optimization_barrier((strips, column))
    pieces = spread_out(raw, "tile")
    strips = [block for strip in strips for block in (strip, swapped(strip, "tile", 1))]
    weighted = on_device(
        functools.partial(spectrum_kernel, count),
        [tile],
        [*strips, column, partial, ctf, col, row],
        [],
        [
            pltpu.VMEM((count * STRIP, width_cols), bf16),
            pltpu.VMEM((2, *quads), f32),
            pltpu.VMEM((2, *quads), f32),
            pltpu.VMEM((2, *plane), f32),
        ],
        jax.ShapeDtypeStruct((2, 4, *plane), f32),
        14 * pass_flops,
    )
    pieces, weighted = lax.optimization_barrier((pieces, weighted))
    scores = on_device(
        functools.partial(score_kernel, count),
        [tile],
        [*pieces, weighted, shape, moment, col, deep, back, out, row_sum, col_sum],
        [],
        [pltpu.VMEM(quads, f32), pltpu.VMEM((2, *quads), bf16)],
        jax.ShapeDtypeStruct((2 * orient_count, mine, STRIP // orient_count, OUTC), bf16),
        12 * pass_flops,
    )
    chips = [[first + k for k in range(2 * orient_count)] for first in range(0, count * orient_count, 2 * orient_count)]
    received = lax.all_to_all(
        scores, ("tile", "orient"), split_axis=0, concat_axis=0, tiled=True, axis_index_groups=chips
    ).astype(f32)
    orient_total = tpl_count * orient_count
    best = jnp.max(received, axis=(0, 1))
    score_mean = jnp.sum(received, axis=(0, 1)) / orient_total
    score_var = jnp.sum(received * received, axis=(0, 1)) / orient_total - score_mean * score_mean
    return (best, (best - score_mean) / jnp.sqrt(score_var + 1e-05))


def solution(mesh):
    placed = (P("tile", None), P("orient", "tile", None), P(), P("tile"))
    return jax.shard_map(
        local,
        mesh=mesh,
        in_specs=placed,
        out_specs=(P(("tile", "orient"), None), P(("tile", "orient"), None)),
        check_vma=False,
    )
```

```python
import functools
import math

import jax
import jax.numpy as jnp
import ml_dtypes
import numpy as np
from jax import lax
from jax.experimental import pallas as pl
from jax.experimental.pallas import tpu as pltpu
from jax.sharding import PartitionSpec as P

TS = 384
STRIP = 256
OUTC = 128
CHUNK = 16
VMEM_BYTES = 24 * 1024 * 1024


def cos_sin(freqs, places, modulus):
    residue = freqs[:, None] * places[None, :] % modulus
    lowest = np.minimum(residue, modulus - residue)
    flipped = np.where(residue > modulus - residue, -1.0, 1.0).astype(np.float32)
    angle = lowest.astype(np.float32) * np.float32(2.0 * math.pi / modulus)
    sine = np.where(2 * lowest == modulus, np.float32(0.0), flipped * np.sin(angle))
    return np.cos(angle).astype(np.float32), sine.astype(np.float32)


def round_up(value, multiple):
    return -(-value // multiple) * multiple


@functools.lru_cache(maxsize=None)
def tables(width_rows, width_cols):
    half = width_cols // 2
    rows = width_rows // 2 + 1
    padded = round_up(rows, CHUNK)
    bf16 = ml_dtypes.bfloat16
    places = np.arange(width_cols)
    cos_v, sin_v = cos_sin(np.arange(half + 1), places, width_cols)
    packed_sin = sin_v[:half].copy()
    forward_sin = -packed_sin
    forward_sin[0] = cos_v[half]
    packed_sin[0] = cos_v[half]
    col = np.concatenate([cos_v[:half], forward_sin], 0).T.astype(bf16)
    back = (2.0 * np.concatenate([cos_v[:half], packed_sin], 0)[:, :OUTC].astype(bf16).astype(np.float32)).astype(bf16)
    cos_u, sin_u = cos_sin(np.arange(rows), np.arange(width_rows), width_rows)
    row = np.zeros((2 * padded, width_rows), np.float32)
    row[:rows] = cos_u
    row[padded : padded + rows] = -sin_u
    row = row.astype(bf16)
    weight = np.ones((rows, 1), np.float32)
    weight[0] = weight[-1] = 0.5
    out = np.zeros((2 * padded, STRIP), np.float32)
    out[:rows] = cos_u[:, :STRIP].astype(bf16).astype(np.float32) * weight
    out[padded : padded + rows] = sin_u[:, :STRIP].astype(bf16).astype(np.float32) * weight
    out = np.ascontiguousarray(out.T).astype(bf16)
    row_sum = row[:, :TS].astype(np.float32).sum(1, keepdims=True)
    col_sum = col[:TS].astype(np.float32).sum(0, keepdims=True)
    return col, row, back, out, row_sum, col_sum


def swapped(value, axis, step):
    count = lax.axis_size(axis)
    return lax.ppermute(value, axis, [(source, source ^ step) for source in range(count)])


def spread_out(value, axis):
    held, step = {0: value}, lax.axis_size(axis) // 2
    while step > 1:
        held |= {index ^ step: swapped(block, axis, step) for index, block in held.items()}
        step //= 2
    return [held[index] for index in sorted(held)[1:]]


def with_partners(blocks, axis):
    return [block for held in blocks for block in (held, swapped(held, axis, 1))]


def dot(left, right):
    return jnp.dot(left, right, preferred_element_type=jnp.float32)


def first_column(shape):
    return lax.broadcasted_iota(jnp.int32, shape, 1) == 0


def quadrants(load, r, padded, half, first):
    up, down = load(slice(r, r + CHUNK)), load(slice(padded + r, padded + r + CHUNK))
    cc, cs, sc, ss = up[:, :half], up[:, half:], down[:, :half], down[:, half:]
    plus_re = cc - jnp.where(first, 0.0, ss)
    plus_im = jnp.where(first, 0.0, cs) + sc
    minus_re = jnp.where(first, cs, cc + ss)
    minus_im = jnp.where(first, ss, cs - sc)
    return plus_re, plus_im, minus_re, minus_im


def template_pair(blocks, bit, raw_ref, index):
    depth = blocks[0].shape[1]
    sums = squares = 0.0
    for j in range(2):
        block = blocks[j][index]
        wide = block.astype(jnp.float32)
        sums = sums + jnp.sum(wide, axis=0, keepdims=True)
        squares = squares + jnp.sum(wide * wide, axis=0, keepdims=True)
        start = pl.multiple_of((bit ^ j) * depth, depth)
        raw_ref[index, pl.ds(start, depth), :] = block.astype(raw_ref.dtype)
    return sums, squares


def ctf_kernel(half, width_rows, tile_ref, group_a, group_b, defocus_ref, ctf_ref):
    padded = ctf_ref.shape[2]
    u = lax.broadcasted_iota(jnp.int32, (8, round_up(padded, 128)), 1).astype(jnp.float32) / width_rows
    column = lax.broadcasted_iota(jnp.int32, (8, half), 1)
    wrapped = (lax.broadcasted_iota(jnp.int32, (8, half), 0) == 1) & (column == 0)
    v = jnp.where(wrapped, half, column).astype(jnp.float32) / (2 * half)
    for k in range(2):
        group = jnp.where((tile_ref[0] & 1) == k, group_a[0], group_b[0])
        turn = jnp.float32(math.pi) * defocus_ref[group]
        phase_u, phase_v = turn * (u * u) + 0.07, turn * (v * v)
        sin_u, cos_u = jnp.sin(phase_u).T[:padded, :1], jnp.cos(phase_u).T[:padded, :1]
        sin_v, cos_v = jnp.sin(phase_v), jnp.cos(phase_v)
        for r in range(0, padded, CHUNK):
            up = slice(r, r + CHUNK)
            for side in range(2):
                row = slice(side, side + 1)
                ctf_ref[k, side, up] = -(sin_u[up] * cos_v[row] + cos_u[up] * sin_v[row])


def template_pair(blocks, bit, raw_ref, index, mine):
    depth = blocks[0].shape[1]
    sums = squares = 0.0
    for j in range(2):
        block = blocks[j][bit * mine + index]
        wide = block.astype(jnp.float32)
        sums = sums + jnp.sum(wide, axis=0, keepdims=True)
        squares = squares + jnp.sum(wide * wide, axis=0, keepdims=True)
        start = pl.multiple_of((bit ^ j) * depth, depth)
        raw_ref[pl.ds(start, depth), :] = block.astype(raw_ref.dtype)
    return sums, squares


def early_kernel(
    tile_ref, strip_a, strip_b, tpl_a, tpl_b, col_ref, row_ref, deep_ref,
    column_ref, *outs
):
    tile = tile_ref[0]
    bit = tile & 1
    shape_ref, moment_ref, raw_ref = outs[-3:]
    for j, strip in enumerate((strip_a, strip_b)):
        start = pl.multiple_of((bit ^ j) * STRIP, STRIP)
        column_ref[pl.ds(start, STRIP), :] = dot(strip[...], col_ref[...]).astype(jnp.bfloat16)
    if len(outs) == 4:
        outs[0][0] = dot(row_ref[:, : 2 * STRIP], column_ref[...])
        outs[0][1] = dot(row_ref[:, :STRIP], column_ref[STRIP:, :])
    else:
        stage_kernel(0, tile_ref, column_ref, row_ref, *outs[:2])
    mine = shape_ref.shape[0]
    for index in range(mine):
        for k, moment in enumerate(template_pair((tpl_a, tpl_b), bit, raw_ref, index, mine)):
            moment_ref[2 * index + k : 2 * index + k + 1, :] = moment
        columns = dot(raw_ref[...].astype(jnp.bfloat16), col_ref[:TS, :]).astype(jnp.bfloat16)
        shape_ref[index] = dot(deep_ref[tile >> 1], columns)


def rows_of(pair, offset, length):
    return pl.ds(pl.multiple_of(pair * (2 * STRIP), 2 * STRIP) + offset, length)


def add_power(power_ref, loads, half, first, fresh):
    padded = power_ref.shape[1]
    for r in range(0, padded, CHUNK):
        up = slice(r, r + CHUNK)
        plus = 0.0 if fresh else power_ref[0, up]
        minus = 0.0 if fresh else power_ref[1, up]
        for load in loads:
            signs = quadrants(load, r, padded, half, first)
            plus = plus + (signs[0] * signs[0] + signs[1] * signs[1])
            minus = minus + (signs[2] * signs[2] + signs[3] * signs[3])
        power_ref[0, up] = plus
        power_ref[1, up] = minus


def other_kernel(count, tile_ref, *refs):
    others = refs[: count - 2]
    column_ref, col_ref, row_ref, part_ref, power_ref, work_ref = refs[count - 2 :]
    half, width_rows = col_ref.shape[1] // 2, row_ref.shape[1]
    tile = tile_ref[0]
    own, pairs = tile >> 1, count // 2
    first = first_column((CHUNK, half))
    for j in range(2, count):
        start = pl.multiple_of((tile ^ j) * STRIP, STRIP)
        part_ref[pl.ds(start, STRIP), :] = dot(others[j - 2][...], col_ref[...]).astype(jnp.bfloat16)
    part_ref[rows_of(own, 0, 2 * STRIP), :] = column_ref[...]
    for j in range(1, pairs):
        pair = own ^ j

        @pl.when(pair + 1 < pairs)
        def _():
            work_ref[0] = dot(row_ref[...], part_ref[rows_of(pair, 0, width_rows), :])
            work_ref[1] = dot(row_ref[...], part_ref[rows_of(pair, STRIP, width_rows), :])

        @pl.when(pair + 1 == pairs)
        def _():
            work_ref[0] = dot(row_ref[:, : 2 * STRIP], part_ref[rows_of(pair, 0, 2 * STRIP), :])
            work_ref[1] = dot(row_ref[:, :STRIP], part_ref[rows_of(pair, STRIP, STRIP), :])

        add_power(power_ref, [lambda s, k=k: work_ref[k, s] for k in range(2)], half, first, j == 1)
    if pairs == 1:
        power_ref[...] = jnp.zeros(power_ref.shape, jnp.float32)


def own_kernel(count, tile_ref, part_ref, partial_ref, others_ref, ctf_ref, row_ref, weighted_ref, cross_ref, power_ref):
    padded, half = power_ref.shape[1:]
    width_rows, width_cols = row_ref.shape[1], 2 * half
    own, pairs = tile_ref[0] >> 1, count // 2
    first = first_column((CHUNK, half))

    def finish(loads):
        total = jnp.zeros((CHUNK, half), jnp.float32)
        for r in range(0, padded, CHUNK):
            up = slice(r, r + CHUNK)
            plus, minus = others_ref[0, up], others_ref[1, up]
            for load in loads:
                signs = quadrants(load, r, padded, half, first)
                plus = plus + (signs[0] * signs[0] + signs[1] * signs[1])
                minus = minus + (signs[2] * signs[2] + signs[3] * signs[3])
            power_ref[0, up] = plus
            power_ref[1, up] = minus
            total = total + (plus + minus)
        last = width_rows // 2
        ends = [power_ref[0, r : r + 1] + power_ref[1, r : r + 1] for r in (0, last)]
        whole = 2.0 * jnp.sum(total, keepdims=True) - jnp.sum(ends[0] + ends[1], keepdims=True)
        mean = whole / (count * width_rows * width_cols)
        for r in range(0, padded, CHUNK):
            up = slice(r, r + CHUNK)
            gains = [lax.rsqrt(power_ref[k, up] * (1.0 / count) + mean) for k in range(2)]
            for k, load in enumerate(loads):
                signs = quadrants(load, r, padded, half, first)
                for side in range(2):
                    gain = gains[side] * ctf_ref[k, side, up]
                    weighted_ref[k, 2 * side, up] = signs[2 * side] * gain
                    weighted_ref[k, 2 * side + 1, up] = signs[2 * side + 1] * gain

    @pl.when(own + 1 < pairs)
    def _():
        cross_ref[0] = dot(row_ref[:, 2 * STRIP :], part_ref[rows_of(own + 1, 0, width_rows - 2 * STRIP), :])
        cross_ref[1] = dot(row_ref[:, STRIP:], part_ref[rows_of(own + 1, 0, width_rows - STRIP), :])
        finish([lambda s, k=k: partial_ref[k, s] + cross_ref[k, s] for k in range(2)])

    @pl.when(own + 1 == pairs)
    def _():
        finish([lambda s, k=k: partial_ref[k, s] for k in range(2)])


def span(strip, blocks):
    start = max(strip, blocks[0])
    stop = min((strip + 1) * STRIP + TS, (blocks[-1] + 1) * STRIP)
    return slice(start * STRIP - strip * STRIP, stop - strip * STRIP), slice(
        (start - blocks[0]) * STRIP, stop - blocks[0] * STRIP
    )


def reached(blocks):
    return [s for s in range(4) if s <= blocks[-1] and (s + 1) * STRIP + TS > blocks[0] * STRIP]


def sources(tile):
    sets = [[tile & 2, tile & 2 | 1], [tile ^ 2], [tile ^ 3]]
    strips = [reached(blocks) for blocks in sets]
    return sets, strips, [[k for k in range(3) if s in strips[k]] for s in range(4)]


def summed(refs, strip, which):
    def load(rows):
        parts = [refs[k][strip, rows] for k in which]
        return functools.reduce(lambda left, right: left + right, parts)

    return load


def gather_power(source_ref, power_ref, loads, half, first):
    for r in range(0, power_ref.shape[1], CHUNK):
        up = slice(r, r + CHUNK)
        plus, minus = (0.0, 0.0) if source_ref is None else (source_ref[0, up], source_ref[1, up])
        for load in loads:
            signs = quadrants(load, r, power_ref.shape[1], half, first)
            plus = plus + (signs[0] * signs[0] + signs[1] * signs[1])
            minus = minus + (signs[2] * signs[2] + signs[3] * signs[3])
        if not loads and source_ref is None:
            plus = minus = jnp.zeros((CHUNK, half), jnp.float32)
        power_ref[0, up] = plus
        power_ref[1, up] = minus


def stage_kernel(stage, tile_ref, *refs):
    earlier, refs = refs[:stage], refs[stage:]
    previous, refs = (refs[0], refs[1:]) if stage else (None, refs)
    if stage:
        low_ref, high_ref, row_ref, quad_ref, power_ref, block_ref = refs
        block_ref[: low_ref.shape[0], :] = low_ref[...]
        block_ref[low_ref.shape[0] :, :] = high_ref[...]
    else:
        block_ref, row_ref, quad_ref, power_ref = refs
    half = quad_ref.shape[2] // 2
    first = first_column((CHUNK, half))
    quads = [*earlier, quad_ref]
    for case in range(4):

        @pl.when(tile_ref[0] == case)
        def _():
            sets, strips, needs = sources(case)
            for s in strips[stage]:
                columns, rows = span(s, sets[stage])
                quad_ref[s] = dot(row_ref[:, columns], block_ref[rows, :])
            done = [s for s in range(4) if max(needs[s]) == stage]
            gather_power(previous, power_ref, [summed(quads, s, needs[s]) for s in done], half, first)


def column_kernel(strip_ref, col_ref, *halves):
    size = halves[0].shape[0]
    for k, half_ref in enumerate(halves):
        half_ref[...] = dot(strip_ref[k * size : (k + 1) * size, :], col_ref[...]).astype(jnp.bfloat16)


def whiten_kernel(tile_ref, first_ref, second_ref, third_ref, power_ref, ctf_ref, weighted_ref):
    padded, half = power_ref.shape[1:]
    width_rows, width_cols = STRIP + TS, 2 * half
    first = first_column((CHUNK, half))
    total = jnp.zeros((CHUNK, half), jnp.float32)
    for r in range(0, padded, CHUNK):
        total = total + (power_ref[0, r : r + CHUNK] + power_ref[1, r : r + CHUNK])
    last = width_rows // 2
    ends = [power_ref[0, r : r + 1] + power_ref[1, r : r + 1] for r in (0, last)]
    whole = 2.0 * jnp.sum(total, keepdims=True) - jnp.sum(ends[0] + ends[1], keepdims=True)
    mean = whole / (4 * width_rows * width_cols)
    for case in range(4):

        @pl.when(tile_ref[0] == case)
        def _():
            needs = sources(case)[2]
            loads = [summed((first_ref, second_ref, third_ref), s, needs[s]) for s in (case & 2, case & 2 | 1)]
            for r in range(0, padded, CHUNK):
                up = slice(r, r + CHUNK)
                gains = [lax.rsqrt(power_ref[k, up] * 0.25 + mean) for k in range(2)]
                for k, load in enumerate(loads):
                    signs = quadrants(load, r, padded, half, first)
                    for side in range(2):
                        gain = gains[side] * ctf_ref[k, side, up]
                        weighted_ref[k, 2 * side, up] = signs[2 * side] * gain
                        weighted_ref[k, 2 * side + 1, up] = signs[2 * side + 1] * gain


def score_kernel(count, tile_ref, *refs):
    others = refs[: count - 2]
    (weighted_ref, shape_ref, moment_ref, col_ref, deep_ref, back_ref, out_ref, row_sum_ref, col_sum_ref) = refs[
        count - 2 : count + 7
    ]
    score_ref, raw_ref, quad_ref, product_ref = refs[count + 7 :]
    padded, half = deep_ref.shape[1] // 2, col_ref.shape[1] // 2
    scale = 1.0 / ((STRIP + TS) * col_ref.shape[0])
    first = first_column((CHUNK, half))
    pieces, mine = score_ref.shape[:2]
    tile = tile_ref[0]
    pairs = count // 2
    for index in range(mine):
        sums, squares = (moment_ref[2 * index + k : 2 * index + k + 1, :] for k in range(2))
        for j in range(1, pairs):
            more = template_pair(others[2 * j - 2 : 2 * j], tile & 1, raw_ref, index, mine)
            sums, squares = sums + more[0], squares + more[1]
            columns = dot(raw_ref[...].astype(jnp.bfloat16), col_ref[:TS, :]).astype(jnp.bfloat16)
            late = dot(deep_ref[(tile >> 1) ^ j], columns)
            quad_ref[...] = late if j == 1 else quad_ref[...] + late
        mean = jnp.sum(sums, keepdims=True) / (TS * TS)
        spread = jnp.sqrt(jnp.sum(squares, keepdims=True) / (TS * TS) - mean * mean + 1e-05)
        col_sum = mean * col_sum_ref[...]

        def load(s):
            known = shape_ref[index, s] + quad_ref[s] if pairs > 1 else shape_ref[index, s]
            return known - row_sum_ref[s, :] * col_sum

        for r in range(0, padded, CHUNK):
            up, down = slice(r, r + CHUNK), slice(padded + r, padded + r + CHUNK)
            a, b, c, d = quadrants(load, r, padded, half, first)
            for k in range(2):
                p, q, s, t = (weighted_ref[k, m, up] for m in range(4))
                plus_re = p * a + q * b
                plus_im = q * a - p * b
                minus_re = s * c + t * d
                minus_im = t * c - s * d
                product_ref[k, up, :half] = (plus_re + jnp.where(first, 0.0, minus_re)).astype(jnp.bfloat16)
                product_ref[k, up, half:] = jnp.where(first, minus_re, -(plus_im + minus_im)).astype(jnp.bfloat16)
                product_ref[k, down, :half] = (jnp.where(first, 0.0, minus_im) - plus_im).astype(jnp.bfloat16)
                product_ref[k, down, half:] = jnp.where(first, -minus_im, minus_re - plus_re).astype(jnp.bfloat16)
        for k in range(2):
            back = dot(product_ref[k], back_ref[...]).astype(jnp.bfloat16)
            score = (dot(out_ref[...], back) * (scale / spread)).reshape(pieces // 2, 2 * STRIP // pieces, OUTC)
            score_ref[k * (pieces // 2) : (k + 1) * (pieces // 2), index] = score.astype(jnp.bfloat16)


def on_device(kernel, scalars, operands, scratch, result, cost):
    vmem, smem = pl.BlockSpec(memory_space=pltpu.VMEM), pl.BlockSpec(memory_space=pltpu.SMEM)
    return pl.pallas_call(
        kernel,
        out_shape=result,
        in_specs=[smem] * len(scalars) + [vmem] * len(operands),
        out_specs=jax.tree.map(lambda _: vmem, result),
        scratch_shapes=scratch,
        compiler_params=pltpu.CompilerParams(vmem_limit_bytes=VMEM_BYTES),
        cost_estimate=None if cost is None else pl.CostEstimate(flops=cost, bytes_accessed=0, transcendentals=0),
    )(*scalars, *operands)


def local(micrograph, templates, defocus, group_of_tile):
    width_cols = micrograph.shape[1]
    width_rows = STRIP + TS
    tpl_count, depth = templates.shape[:2]
    count = lax.axis_size("tile")
    orient_count = lax.axis_size("orient")
    col, row, back, out, row_sum, col_sum = tables(width_rows, width_cols)
    deep = np.stack(np.split(row[:, :TS], count // 2, axis=1))
    padded, half = row.shape[0] // 2, width_cols // 2
    tile = lax.axis_index("tile").astype(jnp.int32).reshape(1)
    plane, quads = (padded, half), (2 * padded, width_cols)
    f32, bf16 = jnp.float32, jnp.bfloat16
    mine = tpl_count // 2
    raw = pltpu.VMEM((2 * depth, TS), bf16 if depth % 16 == 0 else f32)
    pass_flops = 2 * quads[0] * quads[1] * STRIP

    strips = spread_out(micrograph, "tile")
    pieces = spread_out(templates, "tile")
    ctf = on_device(
        functools.partial(ctf_kernel, half, width_rows),
        [tile, group_of_tile, swapped(group_of_tile, "tile", 1), defocus],
        [],
        [],
        jax.ShapeDtypeStruct((2, 2, *plane), f32),
        12 * pass_flops,
    )
    early_in = [micrograph, swapped(micrograph, "tile", 1), templates, swapped(templates, "tile", 1), col, row, deep]
    early_out = [
        jax.ShapeDtypeStruct((mine, *quads), f32),
        jax.ShapeDtypeStruct((round_up(2 * mine, 8), TS), f32),
    ]
    columns_out = jax.ShapeDtypeStruct((2 * STRIP, width_cols), bf16)
    all_quads, power_out = jax.ShapeDtypeStruct((4, *quads), f32), jax.ShapeDtypeStruct((2, *plane), f32)
    weighted_out = jax.ShapeDtypeStruct((2, 4, *plane), f32)
    if count == 4:
        column, quads_0, power, shape, moment = on_device(
            early_kernel, [tile], early_in, [raw], (columns_out, all_quads, power_out, *early_out), None
        )
        strips, power, ctf = lax.optimization_barrier((strips, power, ctf))
        half_out = jax.ShapeDtypeStruct((STRIP // 2, width_cols), bf16)
        block = pltpu.VMEM((STRIP, width_cols), bf16)
        halves = on_device(column_kernel, [], [strips[0], col], [], (half_out, half_out), None)
        received = [swapped(part, "tile", 1) for part in halves]
        quads_1, power = on_device(
            functools.partial(stage_kernel, 1), [tile], [quads_0, power, *halves, row], [block], (all_quads, power_out), None
        )
        quads_2, power = on_device(
            functools.partial(stage_kernel, 2),
            [tile],
            [quads_0, quads_1, power, *received, row],
            [block],
            (all_quads, power_out),
            None,
        )
        pieces, power = lax.optimization_barrier((pieces, power))
        pieces = with_partners(pieces, "tile")
        weighted = on_device(
            whiten_kernel, [tile], [quads_0, quads_1, quads_2, power, ctf], [], weighted_out, None
        )
    else:
        column, partial, shape, moment = on_device(
            early_kernel,
            [tile],
            early_in,
            [raw],
            (columns_out, jax.ShapeDtypeStruct((2, *quads), f32), *early_out),
            None,
        )
        strips, column, ctf = lax.optimization_barrier((strips, column, ctf))
        part, power = on_device(
            functools.partial(other_kernel, count),
            [tile],
            [*with_partners(strips, "tile"), column, col, row],
            [pltpu.VMEM((2, *quads), f32)],
            (jax.ShapeDtypeStruct((count * STRIP, width_cols), bf16), power_out),
            None,
        )
        pieces, power = lax.optimization_barrier((pieces, power))
        pieces = with_partners(pieces, "tile")
        weighted = on_device(
            functools.partial(own_kernel, count),
            [tile],
            [part, partial, power, ctf, row],
            [pltpu.VMEM((2, *quads), f32), pltpu.VMEM((2, *plane), f32)],
            weighted_out,
            None,
        )
    scores = on_device(
        functools.partial(score_kernel, count),
        [tile],
        [*pieces, weighted, shape, moment, col, deep, back, out, row_sum, col_sum],
        [raw, pltpu.VMEM(quads, f32), pltpu.VMEM((2, *quads), bf16)],
        jax.ShapeDtypeStruct((2 * orient_count, mine, STRIP // orient_count, OUTC), bf16),
        None,
    )
    chips = [[first + k for k in range(2 * orient_count)] for first in range(0, count * orient_count, 2 * orient_count)]
    received = lax.all_to_all(
        scores, ("tile", "orient"), split_axis=0, concat_axis=0, tiled=True, axis_index_groups=chips
    ).astype(f32)
    orient_total = tpl_count * orient_count
    best = jnp.max(received, axis=(0, 1))
    score_mean = jnp.sum(received, axis=(0, 1)) / orient_total
    score_var = jnp.sum(received * received, axis=(0, 1)) / orient_total - score_mean * score_mean
    return (best, (best - score_mean) / jnp.sqrt(score_var + 1e-05))


def solution(mesh):
    placed = (P("tile", None), P("orient", "tile", None), P(), P("tile"))
    return jax.shard_map(
        local,
        mesh=mesh,
        in_specs=placed,
        out_specs=(P(("tile", "orient"), None), P(("tile", "orient"), None)),
        check_vma=False,
    )
```

```python
import functools
import math

import jax
import jax.numpy as jnp
import ml_dtypes
import numpy as np
from jax import lax
from jax.experimental import pallas as pl
from jax.experimental.pallas import tpu as pltpu
from jax.sharding import PartitionSpec as P

TS = 384
STRIP = 256
OUTC = 128
CHUNK = 16
LANES = 256
VMEM_BYTES = 24 * 1024 * 1024


def cos_sin(freqs, places, modulus):
    residue = freqs[:, None] * places[None, :] % modulus
    lowest = np.minimum(residue, modulus - residue)
    flipped = np.where(residue > modulus - residue, -1.0, 1.0).astype(np.float32)
    angle = lowest.astype(np.float32) * np.float32(2.0 * math.pi / modulus)
    sine = np.where(2 * lowest == modulus, np.float32(0.0), flipped * np.sin(angle))
    return np.cos(angle).astype(np.float32), sine.astype(np.float32)


def round_up(value, multiple):
    return -(-value // multiple) * multiple


@functools.lru_cache(maxsize=None)
def tables(width_rows, width_cols):
    half = width_cols // 2
    rows = width_rows // 2 + 1
    padded = round_up(rows, CHUNK)
    bf16 = ml_dtypes.bfloat16
    places = np.arange(width_cols)
    cos_v, sin_v = cos_sin(np.arange(half + 1), places, width_cols)
    packed_sin = sin_v[:half].copy()
    forward_sin = -packed_sin
    forward_sin[0] = cos_v[half]
    packed_sin[0] = cos_v[half]
    col = np.concatenate([cos_v[:half], forward_sin], 0).T.astype(bf16)
    back = (2.0 * np.concatenate([cos_v[:half], packed_sin], 0)[:, :OUTC].astype(bf16).astype(np.float32)).astype(bf16)
    cos_u, sin_u = cos_sin(np.arange(rows), np.arange(width_rows), width_rows)
    row = np.zeros((2 * padded, width_rows), np.float32)
    row[:rows] = cos_u
    row[padded : padded + rows] = -sin_u
    row = row.astype(bf16)
    weight = np.ones((rows, 1), np.float32)
    weight[0] = weight[-1] = 0.5
    out = np.zeros((2 * padded, STRIP), np.float32)
    out[:rows] = cos_u[:, :STRIP].astype(bf16).astype(np.float32) * weight
    out[padded : padded + rows] = sin_u[:, :STRIP].astype(bf16).astype(np.float32) * weight
    tall = round_up(padded, 128)
    out = np.concatenate([np.pad(part, ((0, tall - padded), (0, 0))) for part in (out[:padded], out[padded:])])
    out = np.ascontiguousarray(out.T).astype(bf16)
    row_sum = row[:, :TS].astype(np.float32).sum(1, keepdims=True)
    col_sum = col[:TS].astype(np.float32).sum(0, keepdims=True)
    return col, row, back, out, row_sum, col_sum


def swapped(value, axis, step):
    count = lax.axis_size(axis)
    return lax.ppermute(value, axis, [(source, source ^ step) for source in range(count)])


def spread_out(value, axis):
    held, step = {0: value}, lax.axis_size(axis) // 2
    while step > 1:
        held |= {index ^ step: swapped(block, axis, step) for index, block in held.items()}
        step //= 2
    return [held[index] for index in sorted(held)[1:]]


def with_partners(blocks, axis):
    return [block for held in blocks for block in (held, swapped(held, axis, 1))]


def dot(left, right):
    return jnp.dot(left, right, preferred_element_type=jnp.float32)


def tiles(padded, half):
    return [(slice(r, r + CHUNK), lane) for r in range(0, padded, CHUNK) for lane in (0,)]


def lanes(lane):
    return slice(lane, lane + LANES)


def where_first(lane, special, usual):
    if lane:
        return usual
    return jnp.where(lax.broadcasted_iota(jnp.int32, usual.shape, 1) == 0, special, usual)


def quadrants(load, rows, lane, padded, half):
    down = slice(padded + rows.start, padded + rows.stop)
    left, right = lanes(lane), lanes(half + lane)
    cc, cs, sc, ss = load(rows, left), load(rows, right), load(down, left), load(down, right)
    plus_re = cc - where_first(lane, 0.0, ss)
    plus_im = where_first(lane, 0.0, cs) + sc
    minus_re = where_first(lane, cs, cc + ss)
    minus_im = where_first(lane, ss, cs - sc)
    return plus_re, plus_im, minus_re, minus_im


def squared(signs):
    return signs[0] * signs[0] + signs[1] * signs[1], signs[2] * signs[2] + signs[3] * signs[3]


def sum_power(source_ref, power_ref, loads):
    padded, half = power_ref.shape[1:]
    total = 0.0
    for rows, lane in tiles(padded, half):
        at = lanes(lane)
        zero = jnp.zeros((CHUNK, LANES), jnp.float32)
        plus, minus = (zero, zero) if source_ref is None else (source_ref[0, rows, at], source_ref[1, rows, at])
        for load in loads:
            more = squared(quadrants(load, rows, lane, padded, half))
            plus, minus = plus + more[0], minus + more[1]
        power_ref[0, rows, at] = plus
        power_ref[1, rows, at] = minus
        total = total + (plus + minus)
    return total


def mean_power(total, power_ref, count, width_rows):
    last = width_rows // 2
    ends = [power_ref[0, r : r + 1] + power_ref[1, r : r + 1] for r in (0, last)]
    whole = 2.0 * jnp.sum(total, keepdims=True) - jnp.sum(ends[0] + ends[1], keepdims=True)
    return whole / (count * width_rows * 2 * power_ref.shape[2])


def whiten(power_ref, mean, count, ctf_ref, loads, weighted_ref):
    padded, half = power_ref.shape[1:]
    for rows, lane in tiles(padded, half):
        at = lanes(lane)
        gains = [lax.rsqrt(power_ref[side, rows, at] * (1.0 / count) + mean) for side in range(2)]
        for k, load in enumerate(loads):
            signs = quadrants(load, rows, lane, padded, half)
            for side in range(2):
                gain = gains[side] * ctf_ref[k, side, rows, at]
                weighted_ref[k, 2 * side, rows, at] = signs[2 * side] * gain
                weighted_ref[k, 2 * side + 1, rows, at] = signs[2 * side + 1] * gain


def ctf_kernel(half, width_rows, tile_ref, group_a, group_b, defocus_ref, ctf_ref):
    padded = ctf_ref.shape[2]
    u = lax.broadcasted_iota(jnp.int32, (8, round_up(padded, 128)), 1).astype(jnp.float32) / width_rows
    column = lax.broadcasted_iota(jnp.int32, (8, half), 1)
    wrapped = (lax.broadcasted_iota(jnp.int32, (8, half), 0) == 1) & (column == 0)
    v = jnp.where(wrapped, half, column).astype(jnp.float32) / (2 * half)
    for k in range(2):
        group = jnp.where((tile_ref[0] & 1) == k, group_a[0], group_b[0])
        turn = jnp.float32(math.pi) * defocus_ref[group]
        phase_u, phase_v = turn * (u * u) + 0.07, turn * (v * v)
        sin_u, cos_u = jnp.sin(phase_u).T[:padded, :1], jnp.cos(phase_u).T[:padded, :1]
        sin_v, cos_v = jnp.sin(phase_v), jnp.cos(phase_v)
        for r in range(0, padded, CHUNK):
            up = slice(r, r + CHUNK)
            for side in range(2):
                row = slice(side, side + 1)
                ctf_ref[k, side, up] = -(sin_u[up] * cos_v[row] + cos_u[up] * sin_v[row])


def pair_kernel(tile_ref, tpl_a, tpl_b, raw_ref, order_ref):
    bit, depth = tile_ref[0] & 1, tpl_a.shape[1]
    for index in range(raw_ref.shape[0]):
        for j, block in enumerate((tpl_a, tpl_b)):
            rows = pl.ds(pl.multiple_of((bit ^ j) * depth, depth), depth)
            order_ref[index, rows, :] = block[bit * raw_ref.shape[0] + index].astype(order_ref.dtype)
    raw_ref[...] = order_ref[...].astype(raw_ref.dtype)


def moments(block):
    wide = block.astype(jnp.float32)
    return jnp.sum(wide, axis=0, keepdims=True), jnp.sum(wide * wide, axis=0, keepdims=True)


def early_kernel(
    tile_ref, strip_a, strip_b, raw_ref, col_ref, row_ref, deep_ref, column_ref, *outs
):
    tile = tile_ref[0]
    bit = tile & 1
    shape_ref, moment_ref = outs[-2:]
    for j, strip in enumerate((strip_a, strip_b)):
        start = pl.multiple_of((bit ^ j) * STRIP, STRIP)
        column_ref[pl.ds(start, STRIP), :] = dot(strip[...], col_ref[...]).astype(jnp.bfloat16)
    if len(outs) == 3:
        outs[0][0] = dot(row_ref[:, : 2 * STRIP], column_ref[...])
        outs[0][1] = dot(row_ref[:, :STRIP], column_ref[STRIP:, :])
    else:
        stage_kernel(0, tile_ref, column_ref, row_ref, *outs[:2])
    for index in range(shape_ref.shape[0]):
        for k, moment in enumerate(moments(raw_ref[index])):
            moment_ref[2 * index + k : 2 * index + k + 1, :] = moment
        columns = dot(raw_ref[index], col_ref[:TS, :]).astype(jnp.bfloat16)
        shape_ref[index] = dot(deep_ref[tile >> 1], columns)


def rows_of(pair, offset, length):
    return pl.ds(pl.multiple_of(pair * (2 * STRIP), 2 * STRIP) + offset, length)


def other_kernel(count, tile_ref, *refs):
    others = refs[: count - 2]
    column_ref, col_ref, row_ref, part_ref, power_ref, work_ref = refs[count - 2 :]
    width_rows = row_ref.shape[1]
    tile = tile_ref[0]
    own, pairs = tile >> 1, count // 2
    for j in range(2, count):
        start = pl.multiple_of((tile ^ j) * STRIP, STRIP)
        part_ref[pl.ds(start, STRIP), :] = dot(others[j - 2][...], col_ref[...]).astype(jnp.bfloat16)
    part_ref[rows_of(own, 0, 2 * STRIP), :] = column_ref[...]
    for j in range(1, pairs):
        pair = own ^ j

        @pl.when(pair + 1 < pairs)
        def _():
            work_ref[0] = dot(row_ref[...], part_ref[rows_of(pair, 0, width_rows), :])
            work_ref[1] = dot(row_ref[...], part_ref[rows_of(pair, STRIP, width_rows), :])

        @pl.when(pair + 1 == pairs)
        def _():
            work_ref[0] = dot(row_ref[:, : 2 * STRIP], part_ref[rows_of(pair, 0, 2 * STRIP), :])
            work_ref[1] = dot(row_ref[:, :STRIP], part_ref[rows_of(pair, STRIP, STRIP), :])

        loads = [lambda rows, at, k=k: work_ref[k, rows, at] for k in range(2)]
        sum_power(None if j == 1 else power_ref, power_ref, loads)
    if pairs == 1:
        power_ref[...] = jnp.zeros(power_ref.shape, jnp.float32)


def own_kernel(count, tile_ref, part_ref, partial_ref, others_ref, ctf_ref, row_ref, weighted_ref, cross_ref, power_ref):
    width_rows = row_ref.shape[1]
    own, pairs = tile_ref[0] >> 1, count // 2

    def finish(loads):
        total = sum_power(others_ref, power_ref, loads)
        whiten(power_ref, mean_power(total, power_ref, count, width_rows), count, ctf_ref, loads, weighted_ref)

    @pl.when(own + 1 < pairs)
    def _():
        cross_ref[0] = dot(row_ref[:, 2 * STRIP :], part_ref[rows_of(own + 1, 0, width_rows - 2 * STRIP), :])
        cross_ref[1] = dot(row_ref[:, STRIP:], part_ref[rows_of(own + 1, 0, width_rows - STRIP), :])
        finish([lambda rows, at, k=k: partial_ref[k, rows, at] + cross_ref[k, rows, at] for k in range(2)])

    @pl.when(own + 1 == pairs)
    def _():
        finish([lambda rows, at, k=k: partial_ref[k, rows, at] for k in range(2)])


def span(strip, blocks):
    start = max(strip, blocks[0])
    stop = min((strip + 1) * STRIP + TS, (blocks[-1] + 1) * STRIP)
    return slice(start * STRIP - strip * STRIP, stop - strip * STRIP), slice(
        (start - blocks[0]) * STRIP, stop - blocks[0] * STRIP
    )


def reached(blocks):
    return [s for s in range(4) if s <= blocks[-1] and (s + 1) * STRIP + TS > blocks[0] * STRIP]


def sources(tile):
    sets = [[tile & 2, tile & 2 | 1], [tile ^ 2], [tile ^ 3]]
    strips = [reached(blocks) for blocks in sets]
    return sets, strips, [[k for k in range(3) if s in strips[k]] for s in range(4)]


def summed(refs, strip, which):
    def load(rows, at):
        parts = [refs[k][strip, rows, at] for k in which]
        return functools.reduce(lambda left, right: left + right, parts)

    return load


def add_blocks(case, stage, block_ref, row_ref, quad_ref):
    sets, strips, _ = sources(case)
    for s in strips[stage]:
        columns, rows = span(s, sets[stage])
        quad_ref[s] = dot(row_ref[:, columns], block_ref[rows, :])


def stage_kernel(stage, tile_ref, *refs):
    earlier, refs = refs[:stage], refs[stage:]
    if stage:
        previous, strip_ref, col_ref, row_ref, quad_ref, power_ref, block_ref = refs
        block_ref[...] = dot(strip_ref[...], col_ref[...]).astype(jnp.bfloat16)
    else:
        previous, (block_ref, row_ref, quad_ref, power_ref) = None, refs
    quads = [*earlier, quad_ref]
    for case in range(4):

        @pl.when(tile_ref[0] == case)
        def _():
            add_blocks(case, stage, block_ref, row_ref, quad_ref)
            needs = sources(case)[2]
            done = [s for s in range(4) if max(needs[s]) == stage]
            sum_power(previous, power_ref, [summed(quads, s, needs[s]) for s in done])


def last_kernel(
    tile_ref, first_ref, second_ref, previous_ref, strip_ref, col_ref, row_ref, ctf_ref,
    weighted_ref, third_ref, power_ref, block_ref,
):
    block_ref[...] = dot(strip_ref[...], col_ref[...]).astype(jnp.bfloat16)
    quads = [first_ref, second_ref, third_ref]
    for case in range(4):

        @pl.when(tile_ref[0] == case)
        def _():
            add_blocks(case, 2, block_ref, row_ref, third_ref)
            needs = sources(case)[2]
            loads = [summed(quads, s, needs[s]) for s in range(4)]
            total = sum_power(previous_ref, power_ref, [loads[s] for s in range(4) if max(needs[s]) == 2])
            mean = mean_power(total, power_ref, 4, STRIP + TS)
            whiten(power_ref, mean, 4, ctf_ref, loads[case & 2 : (case & 2) + 2], weighted_ref)


def score_kernel(count, tile_ref, *refs):
    pairs = count // 2
    others = refs[: pairs - 1]
    (weighted_ref, shape_ref, moment_ref, col_ref, deep_ref, back_ref, out_ref, row_sum_ref, col_sum_ref) = refs[
        pairs - 1 : pairs + 8
    ]
    score_ref, quad_ref, product_ref, y_ref = refs[pairs + 8 :]
    padded, half = deep_ref.shape[1] // 2, col_ref.shape[1] // 2
    scale = 1.0 / ((STRIP + TS) * col_ref.shape[0])
    pieces, mine = score_ref.shape[:2]
    tile = tile_ref[0]
    tall = y_ref.shape[0] // 2
    for h in range(2):
        y_ref[tall * h + padded : tall * (h + 1), :] = jnp.zeros((tall - padded, 2 * OUTC), jnp.bfloat16)
    for index in range(mine):
        sums, squares = (moment_ref[2 * index + k : 2 * index + k + 1, :] for k in range(2))
        for j in range(1, pairs):
            more = moments(others[j - 1][index])
            sums, squares = sums + more[0], squares + more[1]
            columns = dot(others[j - 1][index], col_ref[:TS, :]).astype(jnp.bfloat16)
            late = dot(deep_ref[(tile >> 1) ^ j], columns)
            quad_ref[...] = late if j == 1 else quad_ref[...] + late
        mean = jnp.sum(sums, keepdims=True) / (TS * TS)
        spread = jnp.sqrt(jnp.sum(squares, keepdims=True) / (TS * TS) - mean * mean + 1e-05)
        col_sum = mean * col_sum_ref[...]

        def load(rows, at):
            known = shape_ref[index, rows, at] + quad_ref[rows, at] if pairs > 1 else shape_ref[index, rows, at]
            return known - row_sum_ref[rows, :] * col_sum[:, at]

        for rows, lane in tiles(padded, half):
            a, b, c, d = quadrants(load, rows, lane, padded, half)
            left, right = lanes(lane), lanes(half + lane)
            for k in range(2):
                p, q, s, t = (weighted_ref[k, m, rows, left] for m in range(4))
                plus_re, plus_im = p * a + q * b, q * a - p * b
                minus_re, minus_im = s * c + t * d, t * c - s * d
                up = slice(2 * k * padded + rows.start, 2 * k * padded + rows.stop)
                down = slice(up.start + padded, up.stop + padded)
                parts = (
                    (up, left, plus_re + where_first(lane, 0.0, minus_re)),
                    (up, right, where_first(lane, minus_re, -(plus_im + minus_im))),
                    (down, left, where_first(lane, 0.0, minus_im) - plus_im),
                    (down, right, where_first(lane, -minus_im, minus_re - plus_re)),
                )
                for height, at, value in parts:
                    product_ref[height, at] = value.astype(jnp.bfloat16)
        back = dot(product_ref[...], back_ref[...]).astype(jnp.bfloat16)
        for k in range(2):
            for h in range(2):
                part = back[(2 * k + h) * padded : (2 * k + h + 1) * padded]
                y_ref[tall * h : tall * h + padded, k * OUTC : (k + 1) * OUTC] = part
        score = dot(out_ref[...], y_ref[...]) * (scale / spread)
        for k in range(2):
            strip = score[:, k * OUTC : (k + 1) * OUTC].reshape(pieces // 2, 2 * STRIP // pieces, OUTC)
            score_ref[k * (pieces // 2) : (k + 1) * (pieces // 2), index] = strip.astype(jnp.bfloat16)


def on_device(kernel, scalars, operands, scratch, result, cost):
    vmem, smem = pl.BlockSpec(memory_space=pltpu.VMEM), pl.BlockSpec(memory_space=pltpu.SMEM)
    return pl.pallas_call(
        kernel,
        out_shape=result,
        in_specs=[smem] * len(scalars) + [vmem] * len(operands),
        out_specs=jax.tree.map(lambda _: vmem, result),
        scratch_shapes=scratch,
        compiler_params=pltpu.CompilerParams(vmem_limit_bytes=VMEM_BYTES),
        cost_estimate=None if cost is None else pl.CostEstimate(flops=cost, bytes_accessed=0, transcendentals=0),
    )(*scalars, *operands)


def local(micrograph, templates, defocus, group_of_tile):
    width_cols = micrograph.shape[1]
    width_rows = STRIP + TS
    tpl_count, depth = templates.shape[:2]
    count = lax.axis_size("tile")
    orient_count = lax.axis_size("orient")
    col, row, back, out, row_sum, col_sum = tables(width_rows, width_cols)
    deep = np.stack(np.split(row[:, :TS], count // 2, axis=1))
    padded, half = row.shape[0] // 2, width_cols // 2
    tile = lax.axis_index("tile").astype(jnp.int32).reshape(1)
    plane, quads = (padded, half), (2 * padded, width_cols)
    f32, bf16 = jnp.float32, jnp.bfloat16
    mine = tpl_count // 2
    pass_flops = 2 * quads[0] * quads[1] * STRIP

    strips = spread_out(micrograph, "tile")
    raw = on_device(
        pair_kernel,
        [tile],
        [templates, swapped(templates, "tile", 1)],
        [pltpu.VMEM((mine, 2 * depth, TS), bf16 if depth % 16 == 0 else f32)],
        jax.ShapeDtypeStruct((mine, 2 * depth, TS), bf16),
        None,
    )
    pieces = spread_out(raw, "tile")
    ctf = on_device(
        functools.partial(ctf_kernel, half, width_rows),
        [tile, group_of_tile, swapped(group_of_tile, "tile", 1), defocus],
        [],
        [],
        jax.ShapeDtypeStruct((2, 2, *plane), f32),
        20 * pass_flops,
    )
    early_in = [micrograph, swapped(micrograph, "tile", 1), raw, col, row, deep]
    early_out = [
        jax.ShapeDtypeStruct((mine, *quads), f32),
        jax.ShapeDtypeStruct((round_up(2 * mine, 8), TS), f32),
    ]
    columns_out = jax.ShapeDtypeStruct((2 * STRIP, width_cols), bf16)
    all_quads, power_out = jax.ShapeDtypeStruct((4, *quads), f32), jax.ShapeDtypeStruct((2, *plane), f32)
    weighted_out = jax.ShapeDtypeStruct((2, 4, *plane), f32)
    if count == 4:
        column, quads_0, power, shape, moment = on_device(
            early_kernel, [tile], early_in, [], (columns_out, all_quads, power_out, *early_out), None
        )
        strips, power, ctf = lax.optimization_barrier((strips, power, ctf))
        block = pltpu.VMEM((STRIP, width_cols), bf16)
        quads_1, power = on_device(
            functools.partial(stage_kernel, 1),
            [tile],
            [quads_0, power, strips[0], col, row],
            [block],
            (all_quads, power_out),
            30 * pass_flops,
        )
        weighted = on_device(
            last_kernel,
            [tile],
            [quads_0, quads_1, power, swapped(strips[0], "tile", 1), col, row, ctf],
            [pltpu.VMEM((4, *quads), f32), pltpu.VMEM((2, *plane), f32), block],
            weighted_out,
            12 * pass_flops,
        )
    else:
        column, partial, shape, moment = on_device(
            early_kernel,
            [tile],
            early_in,
            [],
            (columns_out, jax.ShapeDtypeStruct((2, *quads), f32), *early_out),
            None,
        )
        strips, column, ctf = lax.optimization_barrier((strips, column, ctf))
        part, power = on_device(
            functools.partial(other_kernel, count),
            [tile],
            [*with_partners(strips, "tile"), column, col, row],
            [pltpu.VMEM((2, *quads), f32)],
            (jax.ShapeDtypeStruct((count * STRIP, width_cols), bf16), power_out),
            None,
        )
        weighted = on_device(
            functools.partial(own_kernel, count),
            [tile],
            [part, partial, power, ctf, row],
            [pltpu.VMEM((2, *quads), f32), pltpu.VMEM((2, *plane), f32)],
            weighted_out,
            None,
        )
    scores = on_device(
        functools.partial(score_kernel, count),
        [tile],
        [*pieces, weighted, shape, moment, col, deep, back, out, row_sum, col_sum],
        [
            pltpu.VMEM(quads, f32),
            pltpu.VMEM((4 * padded, width_cols), bf16),
            pltpu.VMEM((out.shape[1], 2 * OUTC), bf16),
        ],
        jax.ShapeDtypeStruct((2 * orient_count, mine, STRIP // orient_count, OUTC), bf16),
        None,
    )
    chips = [[first + k for k in range(2 * orient_count)] for first in range(0, count * orient_count, 2 * orient_count)]
    received = lax.all_to_all(
        scores, ("tile", "orient"), split_axis=0, concat_axis=0, tiled=True, axis_index_groups=chips
    ).astype(f32)
    orient_total = tpl_count * orient_count
    best = jnp.max(received, axis=(0, 1))
    score_mean = jnp.sum(received, axis=(0, 1)) / orient_total
    score_var = jnp.sum(received * received, axis=(0, 1)) / orient_total - score_mean * score_mean
    return (best, (best - score_mean) / jnp.sqrt(score_var + 1e-05))


def solution(mesh):
    placed = (P("tile", None), P("orient", "tile", None), P(), P("tile"))
    return jax.shard_map(
        local,
        mesh=mesh,
        in_specs=placed,
        out_specs=(P(("tile", "orient"), None), P(("tile", "orient"), None)),
        check_vma=False,
    )
```

```python
import functools
import math

import jax
import jax.numpy as jnp
import ml_dtypes
import numpy as np
from jax import lax
from jax.experimental import pallas as pl
from jax.experimental.pallas import tpu as pltpu
from jax.sharding import PartitionSpec as P

TS = 384
STRIP = 256
OUTC = 128
CHUNK = 16
STEP = 8
LANES = 256
VMEM_BYTES = 24 * 1024 * 1024


def cos_sin(freqs, places, modulus):
    residue = freqs[:, None] * places[None, :] % modulus
    lowest = np.minimum(residue, modulus - residue)
    flipped = np.where(residue > modulus - residue, -1.0, 1.0).astype(np.float32)
    angle = lowest.astype(np.float32) * np.float32(2.0 * math.pi / modulus)
    sine = np.where(2 * lowest == modulus, np.float32(0.0), flipped * np.sin(angle))
    return np.cos(angle).astype(np.float32), sine.astype(np.float32)


def round_up(value, multiple):
    return -(-value // multiple) * multiple


@functools.lru_cache(maxsize=None)
def tables(width_rows, width_cols):
    half = width_cols // 2
    rows = width_rows // 2 + 1
    padded = round_up(rows, CHUNK)
    bf16 = ml_dtypes.bfloat16
    places = np.arange(width_cols)
    cos_v, sin_v = cos_sin(np.arange(half + 1), places, width_cols)
    packed_sin = sin_v[:half].copy()
    forward_sin = -packed_sin
    forward_sin[0] = cos_v[half]
    packed_sin[0] = cos_v[half]
    col = np.concatenate([cos_v[:half], forward_sin], 0).T.astype(bf16)
    back = (2.0 * np.concatenate([cos_v[:half], packed_sin], 0)[:, :OUTC].astype(bf16).astype(np.float32)).astype(bf16)
    cos_u, sin_u = cos_sin(np.arange(rows), np.arange(width_rows), width_rows)
    row = np.zeros((2 * padded, width_rows), np.float32)
    row[:rows] = cos_u
    row[padded : padded + rows] = -sin_u
    row = row.astype(bf16)
    weight = np.ones((rows, 1), np.float32)
    weight[0] = weight[-1] = 0.5
    out = np.zeros((2 * padded, STRIP), np.float32)
    out[:rows] = cos_u[:, :STRIP].astype(bf16).astype(np.float32) * weight
    out[padded : padded + rows] = sin_u[:, :STRIP].astype(bf16).astype(np.float32) * weight
    tall = round_up(padded, 128)
    out = np.concatenate([np.pad(part, ((0, tall - padded), (0, 0))) for part in (out[:padded], out[padded:])])
    out = np.ascontiguousarray(out.T).astype(bf16)
    row_sum = row[:, :TS].astype(np.float32).sum(1, keepdims=True)
    col_sum = col[:TS].astype(np.float32).sum(0, keepdims=True)
    return col, row, back, out, row_sum, col_sum


def swapped(value, axis, step):
    count = lax.axis_size(axis)
    return lax.ppermute(value, axis, [(source, source ^ step) for source in range(count)])


def spread_out(value, axis):
    held, step = {0: value}, lax.axis_size(axis) // 2
    while step > 1:
        held |= {index ^ step: swapped(block, axis, step) for index, block in held.items()}
        step //= 2
    return [held[index] for index in sorted(held)[1:]]


def with_partners(blocks, axis):
    return [block for held in blocks for block in (held, swapped(held, axis, 1))]


def dot(left, right):
    return jnp.dot(left, right, preferred_element_type=jnp.float32)


def tiles(padded, half, step):
    return [(slice(r, r + step), lane) for r in range(0, padded, step) for lane in range(0, half, LANES)]


def lanes(lane):
    return slice(lane, lane + LANES)


def where_first(lane, special, usual):
    if lane:
        return usual
    return jnp.where(lax.broadcasted_iota(jnp.int32, usual.shape, 1) == 0, special, usual)


def quadrants(load, rows, lane, padded, half):
    down = slice(padded + rows.start, padded + rows.stop)
    left, right = lanes(lane), lanes(half + lane)
    cc, cs, sc, ss = load(rows, left), load(rows, right), load(down, left), load(down, right)
    plus_re = cc - where_first(lane, 0.0, ss)
    plus_im = where_first(lane, 0.0, cs) + sc
    minus_re = where_first(lane, cs, cc + ss)
    minus_im = where_first(lane, ss, cs - sc)
    return plus_re, plus_im, minus_re, minus_im


def squared(signs):
    return signs[0] * signs[0] + signs[1] * signs[1], signs[2] * signs[2] + signs[3] * signs[3]


def sum_power(source_ref, power_ref, loads):
    padded, half = power_ref.shape[1:]
    total = 0.0
    for rows, lane in tiles(padded, half, STEP):
        at = lanes(lane)
        zero = jnp.zeros((STEP, LANES), jnp.float32)
        plus, minus = (zero, zero) if source_ref is None else (source_ref[0, rows, at], source_ref[1, rows, at])
        for load in loads:
            more = squared(quadrants(load, rows, lane, padded, half))
            plus, minus = plus + more[0], minus + more[1]
        power_ref[0, rows, at] = plus
        power_ref[1, rows, at] = minus
        total = total + (plus + minus)
    return total


def mean_power(total, power_ref, count, width_rows):
    last = width_rows // 2
    ends = [power_ref[0, r : r + 1] + power_ref[1, r : r + 1] for r in (0, last)]
    whole = 2.0 * jnp.sum(total, keepdims=True) - jnp.sum(ends[0] + ends[1], keepdims=True)
    return whole / (count * width_rows * 2 * power_ref.shape[2])


def whiten(power_ref, mean, count, ctf_ref, loads, weighted_ref):
    padded, half = power_ref.shape[1:]
    for rows, lane in tiles(padded, half, STEP):
        at = lanes(lane)
        gains = [lax.rsqrt(power_ref[side, rows, at] * (1.0 / count) + mean) for side in range(2)]
        for k, load in enumerate(loads):
            signs = quadrants(load, rows, lane, padded, half)
            for side in range(2):
                gain = gains[side] * ctf_ref[k, side, rows, at]
                weighted_ref[k, 2 * side, rows, at] = signs[2 * side] * gain
                weighted_ref[k, 2 * side + 1, rows, at] = signs[2 * side + 1] * gain


def ctf_kernel(half, width_rows, tile_ref, group_a, group_b, defocus_ref, ctf_ref):
    padded = ctf_ref.shape[2]
    u = lax.broadcasted_iota(jnp.int32, (8, round_up(padded, 128)), 1).astype(jnp.float32) / width_rows
    column = lax.broadcasted_iota(jnp.int32, (8, half), 1)
    wrapped = (lax.broadcasted_iota(jnp.int32, (8, half), 0) == 1) & (column == 0)
    v = jnp.where(wrapped, half, column).astype(jnp.float32) / (2 * half)
    for k in range(2):
        group = jnp.where((tile_ref[0] & 1) == k, group_a[0], group_b[0])
        turn = jnp.float32(math.pi) * defocus_ref[group]
        phase_u, phase_v = turn * (u * u) + 0.07, turn * (v * v)
        sin_u, cos_u = jnp.sin(phase_u).T[:padded, :1], jnp.cos(phase_u).T[:padded, :1]
        sin_v, cos_v = jnp.sin(phase_v), jnp.cos(phase_v)
        for r in range(0, padded, CHUNK):
            up = slice(r, r + CHUNK)
            for side in range(2):
                row = slice(side, side + 1)
                ctf_ref[k, side, up] = -(sin_u[up] * cos_v[row] + cos_u[up] * sin_v[row])


def pair_kernel(tile_ref, tpl_a, tpl_b, raw_ref, order_ref):
    bit, depth = tile_ref[0] & 1, tpl_a.shape[1]
    for index in range(raw_ref.shape[0]):
        for j, block in enumerate((tpl_a, tpl_b)):
            rows = pl.ds(pl.multiple_of((bit ^ j) * depth, depth), depth)
            order_ref[index, rows, :] = block[bit * raw_ref.shape[0] + index].astype(order_ref.dtype)
    raw_ref[...] = order_ref[...].astype(raw_ref.dtype)


def moments(block):
    wide = block.astype(jnp.float32)
    return jnp.sum(wide, axis=0, keepdims=True), jnp.sum(wide * wide, axis=0, keepdims=True)


def early_kernel(tile_ref, strip_a, strip_b, raw_ref, col_ref, row_ref, deep_ref, *outs):
    tile = tile_ref[0]
    bit = tile & 1
    four = len(outs) == 5
    column_ref = outs[4] if four else outs[0]
    shape_ref, moment_ref = outs[2:4]
    for j, strip in enumerate((strip_a, strip_b)):
        start = pl.multiple_of((bit ^ j) * STRIP, STRIP)
        column_ref[pl.ds(start, STRIP), :] = dot(strip[...], col_ref[...]).astype(jnp.bfloat16)
    if four:
        stage_kernel(0, tile_ref, column_ref, row_ref, *outs[:2])
    else:
        outs[1][0] = dot(row_ref[:, : 2 * STRIP], column_ref[...])
        outs[1][1] = dot(row_ref[:, :STRIP], column_ref[STRIP:, :])
    for index in range(shape_ref.shape[0]):
        for k, moment in enumerate(moments(raw_ref[index])):
            moment_ref[2 * index + k : 2 * index + k + 1, :] = moment
        columns = dot(raw_ref[index], col_ref[:TS, :]).astype(jnp.bfloat16)
        shape_ref[index] = dot(deep_ref[tile >> 1], columns)


def by_case(tile, body):
    def choose(low, high):
        if high - low == 1:
            return body(low)
        middle = (low + high) // 2
        lax.cond(tile < middle, lambda: choose(low, middle), lambda: choose(middle, high))

    choose(0, 4)


def rows_of(pair, offset, length):
    return pl.ds(pl.multiple_of(pair * (2 * STRIP), 2 * STRIP) + offset, length)


def other_kernel(count, tile_ref, *refs):
    others = refs[: count - 2]
    column_ref, col_ref, row_ref, part_ref, power_ref, work_ref = refs[count - 2 :]
    width_rows = row_ref.shape[1]
    tile = tile_ref[0]
    own, pairs = tile >> 1, count // 2
    for j in range(2, count):
        start = pl.multiple_of((tile ^ j) * STRIP, STRIP)
        part_ref[pl.ds(start, STRIP), :] = dot(others[j - 2][...], col_ref[...]).astype(jnp.bfloat16)
    part_ref[rows_of(own, 0, 2 * STRIP), :] = column_ref[...]
    for j in range(1, pairs):
        pair = own ^ j

        @pl.when(pair + 1 < pairs)
        def _():
            work_ref[0] = dot(row_ref[...], part_ref[rows_of(pair, 0, width_rows), :])
            work_ref[1] = dot(row_ref[...], part_ref[rows_of(pair, STRIP, width_rows), :])

        @pl.when(pair + 1 == pairs)
        def _():
            work_ref[0] = dot(row_ref[:, : 2 * STRIP], part_ref[rows_of(pair, 0, 2 * STRIP), :])
            work_ref[1] = dot(row_ref[:, :STRIP], part_ref[rows_of(pair, STRIP, STRIP), :])

        loads = [lambda rows, at, k=k: work_ref[k, rows, at] for k in range(2)]
        sum_power(None if j == 1 else power_ref, power_ref, loads)
    if pairs == 1:
        power_ref[...] = jnp.zeros(power_ref.shape, jnp.float32)


def own_kernel(count, tile_ref, part_ref, partial_ref, others_ref, ctf_ref, row_ref, weighted_ref, cross_ref, power_ref):
    width_rows = row_ref.shape[1]
    own, pairs = tile_ref[0] >> 1, count // 2

    def finish(loads):
        total = sum_power(others_ref, power_ref, loads)
        whiten(power_ref, mean_power(total, power_ref, count, width_rows), count, ctf_ref, loads, weighted_ref)

    @pl.when(own + 1 < pairs)
    def _():
        cross_ref[0] = dot(row_ref[:, 2 * STRIP :], part_ref[rows_of(own + 1, 0, width_rows - 2 * STRIP), :])
        cross_ref[1] = dot(row_ref[:, STRIP:], part_ref[rows_of(own + 1, 0, width_rows - STRIP), :])
        finish([lambda rows, at, k=k: partial_ref[k, rows, at] + cross_ref[k, rows, at] for k in range(2)])

    @pl.when(own + 1 == pairs)
    def _():
        finish([lambda rows, at, k=k: partial_ref[k, rows, at] for k in range(2)])


def span(strip, blocks):
    start = max(strip, blocks[0])
    stop = min((strip + 1) * STRIP + TS, (blocks[-1] + 1) * STRIP)
    return slice(start * STRIP - strip * STRIP, stop - strip * STRIP), slice(
        (start - blocks[0]) * STRIP, stop - blocks[0] * STRIP
    )


def reached(blocks):
    return [s for s in range(4) if s <= blocks[-1] and (s + 1) * STRIP + TS > blocks[0] * STRIP]


def sources(tile):
    sets = [[tile & 2, tile & 2 | 1], [tile ^ 2], [tile ^ 3]]
    strips = [reached(blocks) for blocks in sets]
    return sets, strips, [[k for k in range(3) if s in strips[k]] for s in range(4)]


def view(ref, strip):
    return lambda rows, at: ref[strip, rows, at]


def add_blocks(case, stage, block_ref, row_ref, quads):
    sets, strips, needs = sources(case)
    for s in strips[stage]:
        columns, rows = span(s, sets[stage])
        part = dot(row_ref[:, columns], block_ref[rows, :])
        before = [k for k in needs[s] if k < stage]
        quads[stage][s] = quads[before[-1]][s] + part if before else part


def stage_kernel(stage, tile_ref, *refs):
    earlier, refs = refs[:stage], refs[stage:]
    if stage:
        previous, strip_ref, col_ref, row_ref, quad_ref, power_ref, block_ref = refs
        block_ref[...] = dot(strip_ref[...], col_ref[...]).astype(jnp.bfloat16)
    else:
        previous, (block_ref, row_ref, quad_ref, power_ref) = None, refs
    quads = [*earlier, quad_ref]

    def body(case):
        add_blocks(case, stage, block_ref, row_ref, quads)
        needs = sources(case)[2]
        done = [s for s in range(4) if max(needs[s]) == stage]
        sum_power(previous, power_ref, [view(quads[needs[s][-1]], s) for s in done])

    by_case(tile_ref[0], body)


def last_kernel(
    tile_ref, first_ref, second_ref, previous_ref, strip_ref, col_ref, row_ref, ctf_ref,
    weighted_ref, third_ref, power_ref, block_ref,
):
    block_ref[...] = dot(strip_ref[...], col_ref[...]).astype(jnp.bfloat16)
    quads = [first_ref, second_ref, third_ref]

    def body(case):
        add_blocks(case, 2, block_ref, row_ref, quads)
        needs = sources(case)[2]
        loads = [view(quads[needs[s][-1]], s) for s in range(4)]
        total = sum_power(previous_ref, power_ref, [loads[s] for s in range(4) if max(needs[s]) == 2])
        mean = mean_power(total, power_ref, 4, STRIP + TS)
        whiten(power_ref, mean, 4, ctf_ref, loads[case & 2 : (case & 2) + 2], weighted_ref)

    by_case(tile_ref[0], body)


def score_kernel(count, tile_ref, *refs):
    pairs = count // 2
    others = refs[: pairs - 1]
    (weighted_ref, shape_ref, moment_ref, col_ref, deep_ref, back_ref, out_ref, row_sum_ref, col_sum_ref) = refs[
        pairs - 1 : pairs + 8
    ]
    score_ref, quad_ref, product_ref = refs[pairs + 8 :]
    padded, half = deep_ref.shape[1] // 2, col_ref.shape[1] // 2
    scale = 1.0 / ((STRIP + TS) * col_ref.shape[0])
    pieces, mine = score_ref.shape[:2]
    tile = tile_ref[0]
    tall = product_ref.shape[0] // 2
    for h in range(2):
        product_ref[tall * h + padded : tall * (h + 1), :] = jnp.zeros((tall - padded, 4 * half), jnp.bfloat16)
    for index in range(mine):
        sums, squares = (moment_ref[2 * index + k : 2 * index + k + 1, :] for k in range(2))
        for j in range(1, pairs):
            more = moments(others[j - 1][index])
            sums, squares = sums + more[0], squares + more[1]
            columns = dot(others[j - 1][index], col_ref[:TS, :]).astype(jnp.bfloat16)
            late = dot(deep_ref[(tile >> 1) ^ j], columns)
            quad_ref[...] = late if j == 1 else quad_ref[...] + late
        mean = jnp.sum(sums, keepdims=True) / (TS * TS)
        spread = jnp.sqrt(jnp.sum(squares, keepdims=True) / (TS * TS) - mean * mean + 1e-05)
        col_sum = mean * col_sum_ref[...]

        def load(rows, at):
            known = shape_ref[index, rows, at] + quad_ref[rows, at] if pairs > 1 else shape_ref[index, rows, at]
            return known - row_sum_ref[rows, :] * col_sum[:, at]

        for rows, lane in tiles(padded, half, CHUNK):
            a, b, c, d = quadrants(load, rows, lane, padded, half)
            for k in range(2):
                p, q, s, t = (weighted_ref[k, m, rows, lanes(lane)] for m in range(4))
                plus_re, plus_im = p * a + q * b, q * a - p * b
                minus_re, minus_im = s * c + t * d, t * c - s * d
                up, down = rows, slice(rows.start + tall, rows.stop + tall)
                left, right = lanes(2 * half * k + lane), lanes(2 * half * k + half + lane)
                parts = (
                    (up, left, plus_re + where_first(lane, 0.0, minus_re)),
                    (up, right, where_first(lane, minus_re, -(plus_im + minus_im))),
                    (down, left, where_first(lane, 0.0, minus_im) - plus_im),
                    (down, right, where_first(lane, -minus_im, minus_re - plus_re)),
                )
                for height, at, value in parts:
                    product_ref[height, at] = value.astype(jnp.bfloat16)
        for k in range(2):
            rows_first = dot(out_ref[...], product_ref[:, 2 * half * k : 2 * half * (k + 1)]).astype(jnp.bfloat16)
            score = dot(rows_first, back_ref[...]) * (scale / spread)
            strip = score.reshape(pieces // 2, 2 * STRIP // pieces, OUTC)
            score_ref[k * (pieces // 2) : (k + 1) * (pieces // 2), index] = strip.astype(jnp.bfloat16)


def on_device(kernel, scalars, operands, scratch, result, cost):
    vmem, smem = pl.BlockSpec(memory_space=pltpu.VMEM), pl.BlockSpec(memory_space=pltpu.SMEM)
    return pl.pallas_call(
        kernel,
        out_shape=result,
        in_specs=[smem] * len(scalars) + [vmem] * len(operands),
        out_specs=jax.tree.map(lambda _: vmem, result),
        scratch_shapes=scratch,
        compiler_params=pltpu.CompilerParams(vmem_limit_bytes=VMEM_BYTES),
        cost_estimate=None if cost is None else pl.CostEstimate(flops=cost, bytes_accessed=0, transcendentals=0),
    )(*scalars, *operands)


def local(micrograph, templates, defocus, group_of_tile):
    width_cols = micrograph.shape[1]
    width_rows = STRIP + TS
    tpl_count, depth = templates.shape[:2]
    count = lax.axis_size("tile")
    orient_count = lax.axis_size("orient")
    col, row, back, out, row_sum, col_sum = tables(width_rows, width_cols)
    deep = np.stack(np.split(row[:, :TS], count // 2, axis=1))
    padded, half = row.shape[0] // 2, width_cols // 2
    tile = lax.axis_index("tile").astype(jnp.int32).reshape(1)
    plane, quads = (padded, half), (2 * padded, width_cols)
    f32, bf16 = jnp.float32, jnp.bfloat16
    mine = tpl_count // 2
    pass_flops = 2 * quads[0] * quads[1] * STRIP

    strips = spread_out(micrograph, "tile")
    raw = on_device(
        pair_kernel,
        [tile],
        [templates, swapped(templates, "tile", 1)],
        [pltpu.VMEM((mine, 2 * depth, TS), bf16 if depth % 16 == 0 else f32)],
        jax.ShapeDtypeStruct((mine, 2 * depth, TS), bf16),
        None,
    )
    pieces = spread_out(raw, "tile")
    ctf = on_device(
        functools.partial(ctf_kernel, half, width_rows),
        [tile, group_of_tile, swapped(group_of_tile, "tile", 1), defocus],
        [],
        [],
        jax.ShapeDtypeStruct((2, 2, *plane), f32),
        20 * pass_flops,
    )
    early_in = [micrograph, swapped(micrograph, "tile", 1), raw, col, row, deep]
    early_out = [
        jax.ShapeDtypeStruct((mine, *quads), f32),
        jax.ShapeDtypeStruct((round_up(2 * mine, 8), TS), f32),
    ]
    columns_out = jax.ShapeDtypeStruct((2 * STRIP, width_cols), bf16)
    all_quads, power_out = jax.ShapeDtypeStruct((4, *quads), f32), jax.ShapeDtypeStruct((2, *plane), f32)
    weighted_out = jax.ShapeDtypeStruct((2, 4, *plane), f32)
    if count == 4:
        quads_0, power, shape, moment = on_device(
            early_kernel,
            [tile],
            early_in,
            [pltpu.VMEM(columns_out.shape, bf16)],
            (all_quads, power_out, *early_out),
            None,
        )
        strips, power, ctf = lax.optimization_barrier((strips, power, ctf))
        block = pltpu.VMEM((STRIP, width_cols), bf16)
        quads_1, power = on_device(
            functools.partial(stage_kernel, 1),
            [tile],
            [quads_0, power, strips[0], col, row],
            [block],
            (all_quads, power_out),
            30 * pass_flops,
        )
        weighted = on_device(
            last_kernel,
            [tile],
            [quads_0, quads_1, power, swapped(strips[0], "tile", 1), col, row, ctf],
            [pltpu.VMEM((4, *quads), f32), pltpu.VMEM((2, *plane), f32), block],
            weighted_out,
            12 * pass_flops,
        )
    else:
        column, partial, shape, moment = on_device(
            early_kernel,
            [tile],
            early_in,
            [],
            (columns_out, jax.ShapeDtypeStruct((2, *quads), f32), *early_out),
            None,
        )
        strips, column, ctf = lax.optimization_barrier((strips, column, ctf))
        part, power = on_device(
            functools.partial(other_kernel, count),
            [tile],
            [*with_partners(strips, "tile"), column, col, row],
            [pltpu.VMEM((2, *quads), f32)],
            (jax.ShapeDtypeStruct((count * STRIP, width_cols), bf16), power_out),
            None,
        )
        weighted = on_device(
            functools.partial(own_kernel, count),
            [tile],
            [part, partial, power, ctf, row],
            [pltpu.VMEM((2, *quads), f32), pltpu.VMEM((2, *plane), f32)],
            weighted_out,
            None,
        )
    scores = on_device(
        functools.partial(score_kernel, count),
        [tile],
        [*pieces, weighted, shape, moment, col, deep, back, out, row_sum, col_sum],
        [
            pltpu.VMEM(quads, f32),
            pltpu.VMEM((out.shape[1], 2 * width_cols), bf16),
        ],
        jax.ShapeDtypeStruct((2 * orient_count, mine, STRIP // orient_count, OUTC), bf16),
        None,
    )
    chips = [[first + k for k in range(2 * orient_count)] for first in range(0, count * orient_count, 2 * orient_count)]
    received = lax.all_to_all(
        scores, ("tile", "orient"), split_axis=0, concat_axis=0, tiled=True, axis_index_groups=chips
    ).astype(f32)
    orient_total = tpl_count * orient_count
    best = jnp.max(received, axis=(0, 1))
    score_mean = jnp.sum(received, axis=(0, 1)) / orient_total
    score_var = jnp.sum(received * received, axis=(0, 1)) / orient_total - score_mean * score_mean
    return (best, (best - score_mean) / jnp.sqrt(score_var + 1e-05))


def solution(mesh):
    placed = (P("tile", None), P("orient", "tile", None), P(), P("tile"))
    return jax.shard_map(
        local,
        mesh=mesh,
        in_specs=placed,
        out_specs=(P(("tile", "orient"), None), P(("tile", "orient"), None)),
        check_vma=False,
    )
```

```python
import functools
import math

import jax
import jax.numpy as jnp
import ml_dtypes
import numpy as np
from jax import lax
from jax.experimental import pallas as pl
from jax.experimental.pallas import tpu as pltpu
from jax.sharding import PartitionSpec as P

TS = 384
STRIP = 256
OUTC = 128
CHUNK = 16
STEP = 8
LANES = 256
VMEM_BYTES = 24 * 1024 * 1024


def cos_sin(freqs, places, modulus):
    residue = freqs[:, None] * places[None, :] % modulus
    lowest = np.minimum(residue, modulus - residue)
    flipped = np.where(residue > modulus - residue, -1.0, 1.0).astype(np.float32)
    angle = lowest.astype(np.float32) * np.float32(2.0 * math.pi / modulus)
    sine = np.where(2 * lowest == modulus, np.float32(0.0), flipped * np.sin(angle))
    return np.cos(angle).astype(np.float32), sine.astype(np.float32)


def round_up(value, multiple):
    return -(-value // multiple) * multiple


@functools.lru_cache(maxsize=None)
def tables(width_rows, width_cols):
    half = width_cols // 2
    rows = width_rows // 2 + 1
    padded = round_up(rows, CHUNK)
    bf16 = ml_dtypes.bfloat16
    places = np.arange(width_cols)
    cos_v, sin_v = cos_sin(np.arange(half + 1), places, width_cols)
    packed_sin = sin_v[:half].copy()
    forward_sin = -packed_sin
    forward_sin[0] = cos_v[half]
    packed_sin[0] = cos_v[half]
    col = np.concatenate([cos_v[:half], forward_sin], 0).T.astype(bf16)
    back = (2.0 * np.concatenate([cos_v[:half], packed_sin], 0)[:, :OUTC].astype(bf16).astype(np.float32)).astype(bf16)
    cos_u, sin_u = cos_sin(np.arange(rows), np.arange(width_rows), width_rows)
    row = np.zeros((2 * padded, width_rows), np.float32)
    row[:rows] = cos_u
    row[padded : padded + rows] = -sin_u
    row = row.astype(bf16)
    weight = np.ones((rows, 1), np.float32)
    weight[0] = weight[-1] = 0.5
    out = np.zeros((2 * padded, STRIP), np.float32)
    out[:rows] = cos_u[:, :STRIP].astype(bf16).astype(np.float32) * weight
    out[padded : padded + rows] = sin_u[:, :STRIP].astype(bf16).astype(np.float32) * weight
    tall = round_up(padded, 128)
    out = np.concatenate([np.pad(part, ((0, tall - padded), (0, 0))) for part in (out[:padded], out[padded:])])
    out = np.ascontiguousarray(out.T).astype(bf16)
    row_sum = row[:, :TS].astype(np.float32).sum(1, keepdims=True)
    col_sum = col[:TS].astype(np.float32).sum(0, keepdims=True)
    return col, row, back, out, row_sum, col_sum


def swapped(value, axis, step):
    count = lax.axis_size(axis)
    return lax.ppermute(value, axis, [(source, source ^ step) for source in range(count)])


def spread_out(value, axis):
    held, step = {0: value}, lax.axis_size(axis) // 2
    while step > 1:
        held |= {index ^ step: swapped(block, axis, step) for index, block in held.items()}
        step //= 2
    return [held[index] for index in sorted(held)[1:]]


def with_partners(blocks, axis):
    return [block for held in blocks for block in (held, swapped(held, axis, 1))]


def dot(left, right):
    return jnp.dot(left, right, preferred_element_type=jnp.float32)


def tiles(padded, half, step):
    return [(slice(r, r + step), lane) for r in range(0, padded, step) for lane in range(0, half, LANES)]


def lanes(lane):
    return slice(lane, lane + LANES)


def where_first(lane, special, usual):
    if lane:
        return usual
    return jnp.where(lax.broadcasted_iota(jnp.int32, usual.shape, 1) == 0, special, usual)


def quadrants(load, rows, lane, padded, half):
    down = slice(padded + rows.start, padded + rows.stop)
    left, right = lanes(lane), lanes(half + lane)
    cc, cs, sc, ss = load(rows, left), load(rows, right), load(down, left), load(down, right)
    plus_re = cc - where_first(lane, 0.0, ss)
    plus_im = where_first(lane, 0.0, cs) + sc
    minus_re = where_first(lane, cs, cc + ss)
    minus_im = where_first(lane, ss, cs - sc)
    return plus_re, plus_im, minus_re, minus_im


def squared(signs):
    return signs[0] * signs[0] + signs[1] * signs[1], signs[2] * signs[2] + signs[3] * signs[3]


def sum_power(source_ref, power_ref, loads):
    padded, half = power_ref.shape[1:]
    total = 0.0
    for rows, lane in tiles(padded, half, STEP):
        at = lanes(lane)
        zero = jnp.zeros((STEP, LANES), jnp.float32)
        plus, minus = (zero, zero) if source_ref is None else (source_ref[0, rows, at], source_ref[1, rows, at])
        for load in loads:
            more = squared(quadrants(load, rows, lane, padded, half))
            plus, minus = plus + more[0], minus + more[1]
        power_ref[0, rows, at] = plus
        power_ref[1, rows, at] = minus
        total = total + (plus + minus)
    return total


def mean_power(total, power_ref, count, width_rows):
    last = width_rows // 2
    ends = [power_ref[0, r : r + 1] + power_ref[1, r : r + 1] for r in (0, last)]
    whole = 2.0 * jnp.sum(total, keepdims=True) - jnp.sum(ends[0] + ends[1], keepdims=True)
    return whole / (count * width_rows * 2 * power_ref.shape[2])


def whiten(power_ref, mean, count, ctf_ref, loads, weighted_ref):
    padded, half = power_ref.shape[1:]
    for rows, lane in tiles(padded, half, STEP):
        at = lanes(lane)
        gains = [lax.rsqrt(power_ref[side, rows, at] * (1.0 / count) + mean) for side in range(2)]
        for k, load in enumerate(loads):
            signs = quadrants(load, rows, lane, padded, half)
            for side in range(2):
                gain = gains[side] * ctf_ref[k, side, rows, at]
                weighted_ref[k, 2 * side, rows, at] = signs[2 * side] * gain
                weighted_ref[k, 2 * side + 1, rows, at] = signs[2 * side + 1] * gain


def ctf_kernel(half, width_rows, tile_ref, group_a, group_b, defocus_ref, ctf_ref):
    padded = ctf_ref.shape[2]
    shape_u, shape_v = (8, round_up(padded, 128)), (8, half)
    turns = []
    for k in range(2):
        group = jnp.where((tile_ref[0] & 1) == k, group_a[0], group_b[0])
        turns.append(jnp.float32(math.pi) * defocus_ref[group])

    def turn(shape):
        return jnp.where(lax.broadcasted_iota(jnp.int32, shape, 0) < 2, turns[0], turns[1])

    u = lax.broadcasted_iota(jnp.int32, shape_u, 1).astype(jnp.float32) / width_rows
    column = lax.broadcasted_iota(jnp.int32, shape_v, 1)
    wrapped = ((lax.broadcasted_iota(jnp.int32, shape_v, 0) & 1) == 1) & (column == 0)
    v = jnp.where(wrapped, half, column).astype(jnp.float32) / (2 * half)
    phase_u, phase_v = turn(shape_u) * (u * u) + 0.07, turn(shape_v) * (v * v)
    sin_u, cos_u = jnp.sin(phase_u).T, jnp.cos(phase_u).T
    sin_v, cos_v = jnp.sin(phase_v), jnp.cos(phase_v)
    for k in range(2):
        for r in range(0, padded, CHUNK):
            up, at = slice(r, r + CHUNK), slice(2 * k, 2 * k + 1)
            for side in range(2):
                row = slice(2 * k + side, 2 * k + side + 1)
                ctf_ref[k, side, up] = -(sin_u[up, at] * cos_v[row] + cos_u[up, at] * sin_v[row])


def pair_kernel(tile_ref, tpl_a, tpl_b, raw_ref, order_ref):
    bit, depth = tile_ref[0] & 1, tpl_a.shape[1]
    for index in range(raw_ref.shape[0]):
        for j, block in enumerate((tpl_a, tpl_b)):
            rows = pl.ds(pl.multiple_of((bit ^ j) * depth, depth), depth)
            order_ref[index, rows, :] = block[bit * raw_ref.shape[0] + index].astype(order_ref.dtype)
    raw_ref[...] = order_ref[...].astype(raw_ref.dtype)


def moments(block):
    wide = block.astype(jnp.float32)
    return jnp.sum(wide, axis=0, keepdims=True), jnp.sum(wide * wide, axis=0, keepdims=True)


def early_kernel(tile_ref, strip_a, strip_b, col_ref, row_ref, *outs):
    bit = tile_ref[0] & 1
    four = len(outs) == 3
    column_ref = outs[2] if four else outs[0]
    for j, strip in enumerate((strip_a, strip_b)):
        start = pl.multiple_of((bit ^ j) * STRIP, STRIP)
        column_ref[pl.ds(start, STRIP), :] = dot(strip[...], col_ref[...]).astype(jnp.bfloat16)
    if four:
        stage_kernel(0, tile_ref, column_ref, row_ref, *outs[:2])
    else:
        outs[1][0] = dot(row_ref[:, : 2 * STRIP], column_ref[...])
        outs[1][1] = dot(row_ref[:, :STRIP], column_ref[STRIP:, :])


def shape_kernel(tile_ref, raw_ref, col_ref, deep_ref, shape_ref, moment_ref):
    for index in range(shape_ref.shape[0]):
        for k, moment in enumerate(moments(raw_ref[index])):
            moment_ref[2 * index + k : 2 * index + k + 1, :] = moment
        columns = dot(raw_ref[index], col_ref[:TS, :]).astype(jnp.bfloat16)
        shape_ref[index] = dot(deep_ref[tile_ref[0] >> 1], columns)


def by_case(tile, body):
    def choose(low, high):
        if high - low == 1:
            return body(low)
        middle = (low + high) // 2
        lax.cond(tile < middle, lambda: choose(low, middle), lambda: choose(middle, high))

    choose(0, 4)


def rows_of(pair, offset, length):
    return pl.ds(pl.multiple_of(pair * (2 * STRIP), 2 * STRIP) + offset, length)


def other_kernel(count, tile_ref, *refs):
    others = refs[: count - 2]
    column_ref, col_ref, row_ref, part_ref, power_ref, work_ref = refs[count - 2 :]
    width_rows = row_ref.shape[1]
    tile = tile_ref[0]
    own, pairs = tile >> 1, count // 2
    for j in range(2, count):
        start = pl.multiple_of((tile ^ j) * STRIP, STRIP)
        part_ref[pl.ds(start, STRIP), :] = dot(others[j - 2][...], col_ref[...]).astype(jnp.bfloat16)
    part_ref[rows_of(own, 0, 2 * STRIP), :] = column_ref[...]
    for j in range(1, pairs):
        pair = own ^ j

        @pl.when(pair + 1 < pairs)
        def _():
            work_ref[0] = dot(row_ref[...], part_ref[rows_of(pair, 0, width_rows), :])
            work_ref[1] = dot(row_ref[...], part_ref[rows_of(pair, STRIP, width_rows), :])

        @pl.when(pair + 1 == pairs)
        def _():
            work_ref[0] = dot(row_ref[:, : 2 * STRIP], part_ref[rows_of(pair, 0, 2 * STRIP), :])
            work_ref[1] = dot(row_ref[:, :STRIP], part_ref[rows_of(pair, STRIP, STRIP), :])

        loads = [lambda rows, at, k=k: work_ref[k, rows, at] for k in range(2)]
        sum_power(None if j == 1 else power_ref, power_ref, loads)
    if pairs == 1:
        power_ref[...] = jnp.zeros(power_ref.shape, jnp.float32)


def own_kernel(count, tile_ref, part_ref, partial_ref, others_ref, ctf_ref, row_ref, weighted_ref, cross_ref, power_ref):
    width_rows = row_ref.shape[1]
    own, pairs = tile_ref[0] >> 1, count // 2

    def finish(loads):
        total = sum_power(others_ref, power_ref, loads)
        whiten(power_ref, mean_power(total, power_ref, count, width_rows), count, ctf_ref, loads, weighted_ref)

    @pl.when(own + 1 < pairs)
    def _():
        cross_ref[0] = dot(row_ref[:, 2 * STRIP :], part_ref[rows_of(own + 1, 0, width_rows - 2 * STRIP), :])
        cross_ref[1] = dot(row_ref[:, STRIP:], part_ref[rows_of(own + 1, 0, width_rows - STRIP), :])
        finish([lambda rows, at, k=k: partial_ref[k, rows, at] + cross_ref[k, rows, at] for k in range(2)])

    @pl.when(own + 1 == pairs)
    def _():
        finish([lambda rows, at, k=k: partial_ref[k, rows, at] for k in range(2)])


def span(strip, blocks):
    start = max(strip, blocks[0])
    stop = min((strip + 1) * STRIP + TS, (blocks[-1] + 1) * STRIP)
    return slice(start * STRIP - strip * STRIP, stop - strip * STRIP), slice(
        (start - blocks[0]) * STRIP, stop - blocks[0] * STRIP
    )


def reached(blocks):
    return [s for s in range(4) if s <= blocks[-1] and (s + 1) * STRIP + TS > blocks[0] * STRIP]


def sources(tile):
    sets = [[tile & 2, tile & 2 | 1], [tile ^ 2], [tile ^ 3]]
    strips = [reached(blocks) for blocks in sets]
    return sets, strips, [[k for k in range(3) if s in strips[k]] for s in range(4)]


def view(ref, strip):
    return lambda rows, at: ref[strip, rows, at]


def add_blocks(case, stage, block_ref, row_ref, quads):
    sets, strips, needs = sources(case)
    for s in strips[stage]:
        columns, rows = span(s, sets[stage])
        part = dot(row_ref[:, columns], block_ref[rows, :])
        before = [k for k in needs[s] if k < stage]
        quads[stage][s] = quads[before[-1]][s] + part if before else part


def stage_kernel(stage, tile_ref, *refs):
    earlier, refs = refs[:stage], refs[stage:]
    if stage:
        previous, strip_ref, col_ref, row_ref, quad_ref, power_ref, block_ref = refs
        block_ref[...] = dot(strip_ref[...], col_ref[...]).astype(jnp.bfloat16)
    else:
        previous, (block_ref, row_ref, quad_ref, power_ref) = None, refs
    quads = [*earlier, quad_ref]

    def body(case):
        add_blocks(case, stage, block_ref, row_ref, quads)
        needs = sources(case)[2]
        done = [s for s in range(4) if max(needs[s]) == stage]
        sum_power(previous, power_ref, [view(quads[needs[s][-1]], s) for s in done])

    by_case(tile_ref[0], body)


def last_kernel(
    tile_ref, first_ref, second_ref, previous_ref, strip_ref, col_ref, row_ref, ctf_ref,
    weighted_ref, third_ref, power_ref, block_ref,
):
    block_ref[...] = dot(strip_ref[...], col_ref[...]).astype(jnp.bfloat16)
    quads = [first_ref, second_ref, third_ref]

    def body(case):
        add_blocks(case, 2, block_ref, row_ref, quads)
        needs = sources(case)[2]
        loads = [view(quads[needs[s][-1]], s) for s in range(4)]
        total = sum_power(previous_ref, power_ref, [loads[s] for s in range(4) if max(needs[s]) == 2])
        mean = mean_power(total, power_ref, 4, STRIP + TS)
        whiten(power_ref, mean, 4, ctf_ref, loads[case & 2 : (case & 2) + 2], weighted_ref)

    by_case(tile_ref[0], body)


def score_kernel(count, tile_ref, *refs):
    pairs = count // 2
    others = refs[: pairs - 1]
    (weighted_ref, shape_ref, moment_ref, col_ref, deep_ref, back_ref, out_ref, row_sum_ref, col_sum_ref) = refs[
        pairs - 1 : pairs + 8
    ]
    score_ref, quad_ref, product_ref = refs[pairs + 8 :]
    padded, half = deep_ref.shape[1] // 2, col_ref.shape[1] // 2
    scale = 1.0 / ((STRIP + TS) * col_ref.shape[0])
    pieces, mine = score_ref.shape[:2]
    tile = tile_ref[0]
    tall = product_ref.shape[0] // 2
    for h in range(2):
        product_ref[tall * h + padded : tall * (h + 1), :] = jnp.zeros((tall - padded, 4 * half), jnp.bfloat16)
    for index in range(mine):
        sums, squares = (moment_ref[2 * index + k : 2 * index + k + 1, :] for k in range(2))
        for j in range(1, pairs):
            more = moments(others[j - 1][index])
            sums, squares = sums + more[0], squares + more[1]
            columns = dot(others[j - 1][index], col_ref[:TS, :]).astype(jnp.bfloat16)
            late = dot(deep_ref[(tile >> 1) ^ j], columns)
            quad_ref[...] = late if j == 1 else quad_ref[...] + late
        mean = jnp.sum(sums, keepdims=True) / (TS * TS)
        spread = jnp.sqrt(jnp.sum(squares, keepdims=True) / (TS * TS) - mean * mean + 1e-05)
        col_sum = mean * col_sum_ref[...]

        def load(rows, at):
            known = shape_ref[index, rows, at] + quad_ref[rows, at] if pairs > 1 else shape_ref[index, rows, at]
            return known - row_sum_ref[rows, :] * col_sum[:, at]

        for rows, lane in tiles(padded, half, CHUNK):
            a, b, c, d = quadrants(load, rows, lane, padded, half)
            for k in range(2):
                p, q, s, t = (weighted_ref[k, m, rows, lanes(lane)] for m in range(4))
                plus_re, plus_im = p * a + q * b, q * a - p * b
                minus_re, minus_im = s * c + t * d, t * c - s * d
                up, down = rows, slice(rows.start + tall, rows.stop + tall)
                left, right = lanes(2 * half * k + lane), lanes(2 * half * k + half + lane)
                parts = (
                    (up, left, plus_re + where_first(lane, 0.0, minus_re)),
                    (up, right, where_first(lane, minus_re, -(plus_im + minus_im))),
                    (down, left, where_first(lane, 0.0, minus_im) - plus_im),
                    (down, right, where_first(lane, -minus_im, minus_re - plus_re)),
                )
                for height, at, value in parts:
                    product_ref[height, at] = value.astype(jnp.bfloat16)
        for k in range(2):
            rows_first = dot(out_ref[...], product_ref[:, 2 * half * k : 2 * half * (k + 1)]).astype(jnp.bfloat16)
            score = dot(rows_first, back_ref[...]) * (scale / spread)
            strip = score.reshape(pieces // 2, 2 * STRIP // pieces, OUTC)
            score_ref[k * (pieces // 2) : (k + 1) * (pieces // 2), index] = strip.astype(jnp.bfloat16)


def on_device(kernel, scalars, operands, scratch, result, cost):
    vmem, smem = pl.BlockSpec(memory_space=pltpu.VMEM), pl.BlockSpec(memory_space=pltpu.SMEM)
    return pl.pallas_call(
        kernel,
        out_shape=result,
        in_specs=[smem] * len(scalars) + [vmem] * len(operands),
        out_specs=jax.tree.map(lambda _: vmem, result),
        scratch_shapes=scratch,
        compiler_params=pltpu.CompilerParams(vmem_limit_bytes=VMEM_BYTES),
        cost_estimate=None if cost is None else pl.CostEstimate(flops=cost, bytes_accessed=0, transcendentals=0),
    )(*scalars, *operands)


def local(micrograph, templates, defocus, group_of_tile):
    width_cols = micrograph.shape[1]
    width_rows = STRIP + TS
    tpl_count, depth = templates.shape[:2]
    count = lax.axis_size("tile")
    orient_count = lax.axis_size("orient")
    col, row, back, out, row_sum, col_sum = tables(width_rows, width_cols)
    deep = np.stack(np.split(row[:, :TS], count // 2, axis=1))
    padded, half = row.shape[0] // 2, width_cols // 2
    tile = lax.axis_index("tile").astype(jnp.int32).reshape(1)
    plane, quads = (padded, half), (2 * padded, width_cols)
    f32, bf16 = jnp.float32, jnp.bfloat16
    mine = tpl_count // 2
    pass_flops = 2 * quads[0] * quads[1] * STRIP

    strips = spread_out(micrograph, "tile")
    raw = on_device(
        pair_kernel,
        [tile],
        [templates, swapped(templates, "tile", 1)],
        [pltpu.VMEM((mine, 2 * depth, TS), bf16 if depth % 16 == 0 else f32)],
        jax.ShapeDtypeStruct((mine, 2 * depth, TS), bf16),
        None,
    )
    ctf = on_device(
        functools.partial(ctf_kernel, half, width_rows),
        [tile, group_of_tile, swapped(group_of_tile, "tile", 1), defocus],
        [],
        [],
        jax.ShapeDtypeStruct((2, 2, *plane), f32),
        20 * pass_flops,
    )
    early_in = [micrograph, swapped(micrograph, "tile", 1), col, row]
    shape_out = (
        jax.ShapeDtypeStruct((mine, *quads), f32),
        jax.ShapeDtypeStruct((round_up(2 * mine, 8), TS), f32),
    )
    columns_out = jax.ShapeDtypeStruct((2 * STRIP, width_cols), bf16)
    all_quads, power_out = jax.ShapeDtypeStruct((4, *quads), f32), jax.ShapeDtypeStruct((2, *plane), f32)
    weighted_out = jax.ShapeDtypeStruct((2, 4, *plane), f32)
    if count == 4:
        shape, moment = on_device(shape_kernel, [tile], [raw, col, deep], [], shape_out, None)
        early_in[0], shape = lax.optimization_barrier((early_in[0], shape))
        pieces = spread_out(raw, "tile")
        quads_0, power = on_device(
            early_kernel,
            [tile],
            early_in,
            [pltpu.VMEM(columns_out.shape, bf16)],
            (all_quads, power_out),
            None,
        )
        strips, power, ctf, shape = lax.optimization_barrier((strips, power, ctf, shape))
        block = pltpu.VMEM((STRIP, width_cols), bf16)
        quads_1, power = on_device(
            functools.partial(stage_kernel, 1),
            [tile],
            [quads_0, power, strips[0], col, row],
            [block],
            (all_quads, power_out),
            30 * pass_flops,
        )
        weighted = on_device(
            last_kernel,
            [tile],
            [quads_0, quads_1, power, swapped(strips[0], "tile", 1), col, row, ctf],
            [pltpu.VMEM((4, *quads), f32), pltpu.VMEM((2, *plane), f32), block],
            weighted_out,
            12 * pass_flops,
        )
    else:
        column, partial = on_device(
            early_kernel,
            [tile],
            early_in,
            [],
            (columns_out, jax.ShapeDtypeStruct((2, *quads), f32)),
            None,
        )
        pieces = spread_out(raw, "tile")
        shape, moment = on_device(shape_kernel, [tile], [raw, col, deep], [], shape_out, None)
        strips, column, ctf = lax.optimization_barrier((strips, column, ctf))
        part, power = on_device(
            functools.partial(other_kernel, count),
            [tile],
            [*with_partners(strips, "tile"), column, col, row],
            [pltpu.VMEM((2, *quads), f32)],
            (jax.ShapeDtypeStruct((count * STRIP, width_cols), bf16), power_out),
            None,
        )
        weighted = on_device(
            functools.partial(own_kernel, count),
            [tile],
            [part, partial, power, ctf, row],
            [pltpu.VMEM((2, *quads), f32), pltpu.VMEM((2, *plane), f32)],
            weighted_out,
            None,
        )
    scores = on_device(
        functools.partial(score_kernel, count),
        [tile],
        [*pieces, weighted, shape, moment, col, deep, back, out, row_sum, col_sum],
        [
            pltpu.VMEM(quads, f32),
            pltpu.VMEM((out.shape[1], 2 * width_cols), bf16),
        ],
        jax.ShapeDtypeStruct((2 * orient_count, mine, STRIP // orient_count, OUTC), bf16),
        None,
    )
    chips = [[first + k for k in range(2 * orient_count)] for first in range(0, count * orient_count, 2 * orient_count)]
    received = lax.all_to_all(
        scores, ("tile", "orient"), split_axis=0, concat_axis=0, tiled=True, axis_index_groups=chips
    ).astype(f32)
    orient_total = tpl_count * orient_count
    best = jnp.max(received, axis=(0, 1))
    score_mean = jnp.sum(received, axis=(0, 1)) / orient_total
    score_var = jnp.sum(received * received, axis=(0, 1)) / orient_total - score_mean * score_mean
    return (best, (best - score_mean) / jnp.sqrt(score_var + 1e-05))


def solution(mesh):
    placed = (P("tile", None), P("orient", "tile", None), P(), P("tile"))
    return jax.shard_map(
        local,
        mesh=mesh,
        in_specs=placed,
        out_specs=(P(("tile", "orient"), None), P(("tile", "orient"), None)),
        check_vma=False,
    )
```

```python
import functools
import math

import jax
import jax.numpy as jnp
import ml_dtypes
import numpy as np
from jax import lax
from jax.experimental import pallas as pl
from jax.experimental.pallas import tpu as pltpu
from jax.sharding import PartitionSpec as P

TS = 384
STRIP = 256
OUTC = 128
CHUNK = 16
STEP = 8
LANES = 256
VMEM_BYTES = 24 * 1024 * 1024


def cos_sin(freqs, places, modulus):
    residue = freqs[:, None] * places[None, :] % modulus
    lowest = np.minimum(residue, modulus - residue)
    flipped = np.where(residue > modulus - residue, -1.0, 1.0).astype(np.float32)
    angle = lowest.astype(np.float32) * np.float32(2.0 * math.pi / modulus)
    sine = np.where(2 * lowest == modulus, np.float32(0.0), flipped * np.sin(angle))
    return np.cos(angle).astype(np.float32), sine.astype(np.float32)


def round_up(value, multiple):
    return -(-value // multiple) * multiple


@functools.lru_cache(maxsize=None)
def tables(width_rows, width_cols):
    half = width_cols // 2
    rows = width_rows // 2 + 1
    padded = round_up(rows, CHUNK)
    bf16 = ml_dtypes.bfloat16
    places = np.arange(width_cols)
    cos_v, sin_v = cos_sin(np.arange(half + 1), places, width_cols)
    packed_sin = sin_v[:half].copy()
    forward_sin = -packed_sin
    forward_sin[0] = cos_v[half]
    packed_sin[0] = cos_v[half]
    col = np.concatenate([cos_v[:half], forward_sin], 0).T.astype(bf16)
    back = (2.0 * np.concatenate([cos_v[:half], packed_sin], 0)[:, :OUTC].astype(bf16).astype(np.float32)).astype(bf16)
    cos_u, sin_u = cos_sin(np.arange(rows), np.arange(width_rows), width_rows)
    row = np.zeros((2 * padded, width_rows), np.float32)
    row[:rows] = cos_u
    row[padded : padded + rows] = -sin_u
    row = row.astype(bf16)
    weight = np.ones((rows, 1), np.float32)
    weight[0] = weight[-1] = 0.5
    out = np.zeros((2 * padded, STRIP), np.float32)
    out[:rows] = cos_u[:, :STRIP].astype(bf16).astype(np.float32) * weight
    out[padded : padded + rows] = sin_u[:, :STRIP].astype(bf16).astype(np.float32) * weight
    tall = round_up(padded, 128)
    out = np.concatenate([np.pad(part, ((0, tall - padded), (0, 0))) for part in (out[:padded], out[padded:])])
    out = np.ascontiguousarray(out.T).astype(bf16)
    row_sum = row[:, :TS].astype(np.float32).sum(1, keepdims=True)
    col_sum = col[:TS].astype(np.float32).sum(0, keepdims=True)
    return col, row, back, out, row_sum, col_sum


def swapped(value, axis, step):
    count = lax.axis_size(axis)
    return lax.ppermute(value, axis, [(source, source ^ step) for source in range(count)])


def spread_out(value, axis):
    held, step = {0: value}, lax.axis_size(axis) // 2
    while step > 1:
        held |= {index ^ step: swapped(block, axis, step) for index, block in held.items()}
        step //= 2
    return [held[index] for index in sorted(held)[1:]]


def with_partners(blocks, axis):
    return [block for held in blocks for block in (held, swapped(held, axis, 1))]


def dot(left, right):
    return jnp.dot(left, right, preferred_element_type=jnp.float32)


def tiles(padded, half, step):
    return [(slice(r, r + step), lane) for r in range(0, padded, step) for lane in range(0, half, LANES)]


def lanes(lane):
    return slice(lane, lane + LANES)


def where_first(lane, special, usual):
    if lane:
        return usual
    return jnp.where(lax.broadcasted_iota(jnp.int32, usual.shape, 1) == 0, special, usual)


def quadrants(load, rows, lane, padded, half):
    down = slice(padded + rows.start, padded + rows.stop)
    left, right = lanes(lane), lanes(half + lane)
    cc, cs, sc, ss = load(rows, left), load(rows, right), load(down, left), load(down, right)
    plus_re = cc - where_first(lane, 0.0, ss)
    plus_im = where_first(lane, 0.0, cs) + sc
    minus_re = where_first(lane, cs, cc + ss)
    minus_im = where_first(lane, ss, cs - sc)
    return plus_re, plus_im, minus_re, minus_im


def squared(signs):
    return signs[0] * signs[0] + signs[1] * signs[1], signs[2] * signs[2] + signs[3] * signs[3]


def sum_power(source_ref, power_ref, loads):
    padded, half = power_ref.shape[1:]
    total = 0.0
    for rows, lane in tiles(padded, half, STEP):
        at = lanes(lane)
        zero = jnp.zeros((STEP, LANES), jnp.float32)
        plus, minus = (zero, zero) if source_ref is None else (source_ref[0, rows, at], source_ref[1, rows, at])
        for load in loads:
            more = squared(quadrants(load, rows, lane, padded, half))
            plus, minus = plus + more[0], minus + more[1]
        power_ref[0, rows, at] = plus
        power_ref[1, rows, at] = minus
        total = total + (plus + minus)
    return total


def mean_power(total, power_ref, count, width_rows):
    last = width_rows // 2
    ends = [power_ref[0, r : r + 1] + power_ref[1, r : r + 1] for r in (0, last)]
    whole = 2.0 * jnp.sum(total, keepdims=True) - jnp.sum(ends[0] + ends[1], keepdims=True)
    return whole / (count * width_rows * 2 * power_ref.shape[2])


def whiten(power_ref, mean, count, ctf_ref, loads, weighted_ref):
    padded, half = power_ref.shape[1:]
    for rows, lane in tiles(padded, half, STEP):
        at = lanes(lane)
        gains = [lax.rsqrt(power_ref[side, rows, at] * (1.0 / count) + mean) for side in range(2)]
        for k, load in enumerate(loads):
            signs = quadrants(load, rows, lane, padded, half)
            for side in range(2):
                gain = gains[side] * ctf_ref[k, side, rows, at]
                weighted_ref[k, 2 * side, rows, at] = signs[2 * side] * gain
                weighted_ref[k, 2 * side + 1, rows, at] = signs[2 * side + 1] * gain


def ctf_kernel(half, width_rows, tile_ref, group_a, group_b, defocus_ref, ctf_ref):
    padded = ctf_ref.shape[2]
    shape_u, shape_v = (8, round_up(padded, 128)), (8, half)
    turns = []
    for k in range(2):
        group = jnp.where((tile_ref[0] & 1) == k, group_a[0], group_b[0])
        turns.append(jnp.float32(math.pi) * defocus_ref[group])

    def turn(shape):
        return jnp.where(lax.broadcasted_iota(jnp.int32, shape, 0) < 2, turns[0], turns[1])

    u = lax.broadcasted_iota(jnp.int32, shape_u, 1).astype(jnp.float32) / width_rows
    column = lax.broadcasted_iota(jnp.int32, shape_v, 1)
    wrapped = ((lax.broadcasted_iota(jnp.int32, shape_v, 0) & 1) == 1) & (column == 0)
    v = jnp.where(wrapped, half, column).astype(jnp.float32) / (2 * half)
    phase_u, phase_v = turn(shape_u) * (u * u) + 0.07, turn(shape_v) * (v * v)
    sin_u, cos_u = jnp.sin(phase_u).T, jnp.cos(phase_u).T
    sin_v, cos_v = jnp.sin(phase_v), jnp.cos(phase_v)
    for k in range(2):
        for r in range(0, padded, CHUNK):
            up, at = slice(r, r + CHUNK), slice(2 * k, 2 * k + 1)
            for side in range(2):
                row = slice(2 * k + side, 2 * k + side + 1)
                ctf_ref[k, side, up] = -(sin_u[up, at] * cos_v[row] + cos_u[up, at] * sin_v[row])


def pair_kernel(tile_ref, tpl_a, tpl_b, raw_ref, order_ref):
    bit, depth = tile_ref[0] & 1, tpl_a.shape[1]
    for index in range(raw_ref.shape[0]):
        for j, block in enumerate((tpl_a, tpl_b)):
            rows = pl.ds(pl.multiple_of((bit ^ j) * depth, depth), depth)
            order_ref[index, rows, :] = block[bit * raw_ref.shape[0] + index].astype(order_ref.dtype)
    raw_ref[...] = order_ref[...].astype(raw_ref.dtype)


def moments(block):
    wide = block.astype(jnp.float32)
    return jnp.sum(wide, axis=0, keepdims=True), jnp.sum(wide * wide, axis=0, keepdims=True)


def early_kernel(tile_ref, strip_a, strip_b, col_ref, row_ref, *outs):
    bit = tile_ref[0] & 1
    four = len(outs) == 3
    column_ref = outs[2] if four else outs[0]
    for j, strip in enumerate((strip_a, strip_b)):
        start = pl.multiple_of((bit ^ j) * STRIP, STRIP)
        column_ref[pl.ds(start, STRIP), :] = dot(strip[...], col_ref[...]).astype(jnp.bfloat16)
    if four:
        stage_kernel(0, tile_ref, column_ref, row_ref, *outs[:2])
    else:
        outs[1][0] = dot(row_ref[:, : 2 * STRIP], column_ref[...])
        outs[1][1] = dot(row_ref[:, :STRIP], column_ref[STRIP:, :])


def shape_kernel(tile_ref, raw_ref, col_ref, deep_ref, shape_ref, moment_ref):
    for index in range(shape_ref.shape[0]):
        for k, moment in enumerate(moments(raw_ref[index])):
            moment_ref[2 * index + k : 2 * index + k + 1, :] = moment
        columns = dot(raw_ref[index], col_ref[:TS, :]).astype(jnp.bfloat16)
        shape_ref[index] = dot(deep_ref[tile_ref[0] >> 1], columns)


def by_case(tile, body):
    def choose(low, high):
        if high - low == 1:
            return body(low)
        middle = (low + high) // 2
        lax.cond(tile < middle, lambda: choose(low, middle), lambda: choose(middle, high))

    choose(0, 4)


def rows_of(pair, offset, length):
    return pl.ds(pl.multiple_of(pair * (2 * STRIP), 2 * STRIP) + offset, length)


def other_kernel(count, tile_ref, *refs):
    others = refs[: count - 2]
    column_ref, col_ref, row_ref, part_ref, power_ref, work_ref = refs[count - 2 :]
    width_rows = row_ref.shape[1]
    tile = tile_ref[0]
    own, pairs = tile >> 1, count // 2
    for j in range(2, count):
        start = pl.multiple_of((tile ^ j) * STRIP, STRIP)
        part_ref[pl.ds(start, STRIP), :] = dot(others[j - 2][...], col_ref[...]).astype(jnp.bfloat16)
    part_ref[rows_of(own, 0, 2 * STRIP), :] = column_ref[...]
    for j in range(1, pairs):
        pair = own ^ j

        @pl.when(pair + 1 < pairs)
        def _():
            work_ref[0] = dot(row_ref[...], part_ref[rows_of(pair, 0, width_rows), :])
            work_ref[1] = dot(row_ref[...], part_ref[rows_of(pair, STRIP, width_rows), :])

        @pl.when(pair + 1 == pairs)
        def _():
            work_ref[0] = dot(row_ref[:, : 2 * STRIP], part_ref[rows_of(pair, 0, 2 * STRIP), :])
            work_ref[1] = dot(row_ref[:, :STRIP], part_ref[rows_of(pair, STRIP, STRIP), :])

        loads = [lambda rows, at, k=k: work_ref[k, rows, at] for k in range(2)]
        sum_power(None if j == 1 else power_ref, power_ref, loads)
    if pairs == 1:
        power_ref[...] = jnp.zeros(power_ref.shape, jnp.float32)


def own_kernel(count, tile_ref, part_ref, partial_ref, others_ref, ctf_ref, row_ref, weighted_ref, cross_ref, power_ref):
    width_rows = row_ref.shape[1]
    own, pairs = tile_ref[0] >> 1, count // 2

    def finish(loads):
        total = sum_power(others_ref, power_ref, loads)
        whiten(power_ref, mean_power(total, power_ref, count, width_rows), count, ctf_ref, loads, weighted_ref)

    @pl.when(own + 1 < pairs)
    def _():
        cross_ref[0] = dot(row_ref[:, 2 * STRIP :], part_ref[rows_of(own + 1, 0, width_rows - 2 * STRIP), :])
        cross_ref[1] = dot(row_ref[:, STRIP:], part_ref[rows_of(own + 1, 0, width_rows - STRIP), :])
        finish([lambda rows, at, k=k: partial_ref[k, rows, at] + cross_ref[k, rows, at] for k in range(2)])

    @pl.when(own + 1 == pairs)
    def _():
        finish([lambda rows, at, k=k: partial_ref[k, rows, at] for k in range(2)])


def span(strip, blocks):
    start = max(strip, blocks[0])
    stop = min((strip + 1) * STRIP + TS, (blocks[-1] + 1) * STRIP)
    return slice(start * STRIP - strip * STRIP, stop - strip * STRIP), slice(
        (start - blocks[0]) * STRIP, stop - blocks[0] * STRIP
    )


def reached(blocks):
    return [s for s in range(4) if s <= blocks[-1] and (s + 1) * STRIP + TS > blocks[0] * STRIP]


def sources(tile):
    sets = [[tile & 2, tile & 2 | 1], [tile ^ 2], [tile ^ 3]]
    strips = [reached(blocks) for blocks in sets]
    return sets, strips, [[k for k in range(3) if s in strips[k]] for s in range(4)]


def view(ref, strip):
    return lambda rows, at: ref[strip, rows, at]


def add_blocks(case, stage, block_ref, row_ref, quads):
    sets, strips, needs = sources(case)
    for s in strips[stage]:
        columns, rows = span(s, sets[stage])
        part = dot(row_ref[:, columns], block_ref[rows, :])
        before = [k for k in needs[s] if k < stage]
        quads[stage][s] = quads[before[-1]][s] + part if before else part


def stage_kernel(stage, tile_ref, *refs):
    earlier, refs = refs[:stage], refs[stage:]
    if stage:
        previous, strip_ref, col_ref, row_ref, quad_ref, power_ref, block_ref = refs
        block_ref[...] = dot(strip_ref[...], col_ref[...]).astype(jnp.bfloat16)
    else:
        previous, (block_ref, row_ref, quad_ref, power_ref) = None, refs
    quads = [*earlier, quad_ref]

    def body(case):
        add_blocks(case, stage, block_ref, row_ref, quads)
        needs = sources(case)[2]
        done = [s for s in range(4) if max(needs[s]) == stage]
        sum_power(previous, power_ref, [view(quads[needs[s][-1]], s) for s in done])

    by_case(tile_ref[0], body)


def last_kernel(
    tile_ref, first_ref, second_ref, previous_ref, strip_ref, col_ref, row_ref, ctf_ref,
    weighted_ref, third_ref, power_ref, block_ref,
):
    block_ref[...] = dot(strip_ref[...], col_ref[...]).astype(jnp.bfloat16)
    quads = [first_ref, second_ref, third_ref]

    def body(case):
        add_blocks(case, 2, block_ref, row_ref, quads)
        needs = sources(case)[2]
        loads = [view(quads[needs[s][-1]], s) for s in range(4)]
        total = sum_power(previous_ref, power_ref, [loads[s] for s in range(4) if max(needs[s]) == 2])
        mean = mean_power(total, power_ref, 4, STRIP + TS)
        whiten(power_ref, mean, 4, ctf_ref, loads[case & 2 : (case & 2) + 2], weighted_ref)

    by_case(tile_ref[0], body)


def score_kernel(count, tile_ref, *refs):
    pairs = count // 2
    others = refs[: pairs - 1]
    (weighted_ref, shape_ref, moment_ref, col_ref, deep_ref, back_ref, out_ref, row_sum_ref, col_sum_ref) = refs[
        pairs - 1 : pairs + 8
    ]
    score_ref, quad_ref, product_ref = refs[pairs + 8 :]
    padded, half = deep_ref.shape[1] // 2, col_ref.shape[1] // 2
    scale = 1.0 / ((STRIP + TS) * col_ref.shape[0])
    pieces, mine = 2 * score_ref.shape[0], score_ref.shape[2]
    tile = tile_ref[0]
    tall = product_ref.shape[0] // 2
    for h in range(2):
        product_ref[tall * h + padded : tall * (h + 1), :] = jnp.zeros((tall - padded, 4 * half), jnp.bfloat16)
    for index in range(mine):
        sums, squares = (moment_ref[2 * index + k : 2 * index + k + 1, :] for k in range(2))
        for j in range(1, pairs):
            more = moments(others[j - 1][index])
            sums, squares = sums + more[0], squares + more[1]
            columns = dot(others[j - 1][index], col_ref[:TS, :]).astype(jnp.bfloat16)
            late = dot(deep_ref[(tile >> 1) ^ j], columns)
            quad_ref[...] = late if j == 1 else quad_ref[...] + late
        mean = jnp.sum(sums, keepdims=True) / (TS * TS)
        spread = jnp.sqrt(jnp.sum(squares, keepdims=True) / (TS * TS) - mean * mean + 1e-05)
        col_sum = mean * col_sum_ref[...]

        def load(rows, at):
            known = shape_ref[index, rows, at] + quad_ref[rows, at] if pairs > 1 else shape_ref[index, rows, at]
            return known - row_sum_ref[rows, :] * col_sum[:, at]

        for rows, lane in tiles(padded, half, CHUNK):
            a, b, c, d = quadrants(load, rows, lane, padded, half)
            for k in range(2):
                p, q, s, t = (weighted_ref[k, m, rows, lanes(lane)] for m in range(4))
                plus_re, plus_im = p * a + q * b, q * a - p * b
                minus_re, minus_im = s * c + t * d, t * c - s * d
                up, down = rows, slice(rows.start + tall, rows.stop + tall)
                left, right = lanes(2 * half * k + lane), lanes(2 * half * k + half + lane)
                parts = (
                    (up, left, plus_re + where_first(lane, 0.0, minus_re)),
                    (up, right, where_first(lane, minus_re, -(plus_im + minus_im))),
                    (down, left, where_first(lane, 0.0, minus_im) - plus_im),
                    (down, right, where_first(lane, -minus_im, minus_re - plus_re)),
                )
                for height, at, value in parts:
                    product_ref[height, at] = value.astype(jnp.bfloat16)
        for k in range(2):
            rows_first = dot(out_ref[...], product_ref[:, 2 * half * k : 2 * half * (k + 1)]).astype(jnp.bfloat16)
            score = dot(rows_first, back_ref[...]) * (scale / spread)
            strip = score.reshape(pieces // 2, 2 * STRIP // pieces, OUTC)
            score_ref[:, k, index] = strip.astype(jnp.bfloat16)


def on_device(kernel, scalars, operands, scratch, result, cost):
    vmem, smem = pl.BlockSpec(memory_space=pltpu.VMEM), pl.BlockSpec(memory_space=pltpu.SMEM)
    return pl.pallas_call(
        kernel,
        out_shape=result,
        in_specs=[smem] * len(scalars) + [vmem] * len(operands),
        out_specs=jax.tree.map(lambda _: vmem, result),
        scratch_shapes=scratch,
        compiler_params=pltpu.CompilerParams(vmem_limit_bytes=VMEM_BYTES),
        cost_estimate=None if cost is None else pl.CostEstimate(flops=cost, bytes_accessed=0, transcendentals=0),
    )(*scalars, *operands)


def local(micrograph, templates, defocus, group_of_tile):
    width_cols = micrograph.shape[1]
    width_rows = STRIP + TS
    tpl_count, depth = templates.shape[:2]
    count = lax.axis_size("tile")
    orient_count = lax.axis_size("orient")
    col, row, back, out, row_sum, col_sum = tables(width_rows, width_cols)
    deep = np.stack(np.split(row[:, :TS], count // 2, axis=1))
    padded, half = row.shape[0] // 2, width_cols // 2
    tile = lax.axis_index("tile").astype(jnp.int32).reshape(1)
    plane, quads = (padded, half), (2 * padded, width_cols)
    f32, bf16 = jnp.float32, jnp.bfloat16
    mine = tpl_count // 2
    pass_flops = 2 * quads[0] * quads[1] * STRIP

    strips = spread_out(micrograph, "tile")
    raw = on_device(
        pair_kernel,
        [tile],
        [templates, swapped(templates, "tile", 1)],
        [pltpu.VMEM((mine, 2 * depth, TS), bf16 if depth % 16 == 0 else f32)],
        jax.ShapeDtypeStruct((mine, 2 * depth, TS), bf16),
        None,
    )
    ctf = on_device(
        functools.partial(ctf_kernel, half, width_rows),
        [tile, group_of_tile, swapped(group_of_tile, "tile", 1), defocus],
        [],
        [],
        jax.ShapeDtypeStruct((2, 2, *plane), f32),
        20 * pass_flops,
    )
    early_in = [micrograph, swapped(micrograph, "tile", 1), col, row]
    shape_out = (
        jax.ShapeDtypeStruct((mine, *quads), f32),
        jax.ShapeDtypeStruct((round_up(2 * mine, 8), TS), f32),
    )
    columns_out = jax.ShapeDtypeStruct((2 * STRIP, width_cols), bf16)
    all_quads, power_out = jax.ShapeDtypeStruct((4, *quads), f32), jax.ShapeDtypeStruct((2, *plane), f32)
    weighted_out = jax.ShapeDtypeStruct((2, 4, *plane), f32)
    if count == 4:
        shape, moment = on_device(shape_kernel, [tile], [raw, col, deep], [], shape_out, None)
        early_in[0], shape = lax.optimization_barrier((early_in[0], shape))
        pieces = spread_out(raw, "tile")
        quads_0, power = on_device(
            early_kernel,
            [tile],
            early_in,
            [pltpu.VMEM(columns_out.shape, bf16)],
            (all_quads, power_out),
            None,
        )
        strips, power, ctf, shape = lax.optimization_barrier((strips, power, ctf, shape))
        block = pltpu.VMEM((STRIP, width_cols), bf16)
        quads_1, power = on_device(
            functools.partial(stage_kernel, 1),
            [tile],
            [quads_0, power, strips[0], col, row],
            [block],
            (all_quads, power_out),
            30 * pass_flops,
        )
        weighted = on_device(
            last_kernel,
            [tile],
            [quads_0, quads_1, power, swapped(strips[0], "tile", 1), col, row, ctf],
            [pltpu.VMEM((4, *quads), f32), pltpu.VMEM((2, *plane), f32), block],
            weighted_out,
            12 * pass_flops,
        )
    else:
        column, partial = on_device(
            early_kernel,
            [tile],
            early_in,
            [],
            (columns_out, jax.ShapeDtypeStruct((2, *quads), f32)),
            None,
        )
        pieces = spread_out(raw, "tile")
        shape, moment = on_device(shape_kernel, [tile], [raw, col, deep], [], shape_out, None)
        strips, column, ctf = lax.optimization_barrier((strips, column, ctf))
        part, power = on_device(
            functools.partial(other_kernel, count),
            [tile],
            [*with_partners(strips, "tile"), column, col, row],
            [pltpu.VMEM((2, *quads), f32)],
            (jax.ShapeDtypeStruct((count * STRIP, width_cols), bf16), power_out),
            None,
        )
        weighted = on_device(
            functools.partial(own_kernel, count),
            [tile],
            [part, partial, power, ctf, row],
            [pltpu.VMEM((2, *quads), f32), pltpu.VMEM((2, *plane), f32)],
            weighted_out,
            None,
        )
    scores = on_device(
        functools.partial(score_kernel, count),
        [tile],
        [*pieces, weighted, shape, moment, col, deep, back, out, row_sum, col_sum],
        [
            pltpu.VMEM(quads, f32),
            pltpu.VMEM((out.shape[1], 2 * width_cols), bf16),
        ],
        jax.ShapeDtypeStruct((orient_count, 2, mine, STRIP // orient_count, OUTC), bf16),
        None,
    )
    scores = scores.reshape(2 * orient_count, *scores.shape[2:])
    chips = [
        [(2 * chip + core) * orient_count + orient for orient in range(orient_count) for core in range(2)]
        for chip in range(count // 2)
    ]
    received = lax.all_to_all(
        scores, ("tile", "orient"), split_axis=0, concat_axis=0, tiled=True, axis_index_groups=chips
    ).astype(f32)
    orient_total = tpl_count * orient_count
    best = jnp.max(received, axis=(0, 1))
    score_mean = jnp.sum(received, axis=(0, 1)) / orient_total
    score_var = jnp.sum(received * received, axis=(0, 1)) / orient_total - score_mean * score_mean
    return (best, (best - score_mean) / jnp.sqrt(score_var + 1e-05))


def solution(mesh):
    placed = (P("tile", None), P("orient", "tile", None), P(), P("tile"))
    return jax.shard_map(
        local,
        mesh=mesh,
        in_specs=placed,
        out_specs=(P(("tile", "orient"), None), P(("tile", "orient"), None)),
        check_vma=False,
    )
```

```python
import functools
import math

import jax
import jax.numpy as jnp
import ml_dtypes
import numpy as np
from jax import lax
from jax.experimental import pallas as pl
from jax.experimental.pallas import tpu as pltpu
from jax.sharding import PartitionSpec as P

TS = 384
STRIP = 256
OUTC = 128
CHUNK = 48
STEP = 8
LANES = 256
VMEM_BYTES = 24 * 1024 * 1024


def cos_sin(freqs, places, modulus):
    residue = freqs[:, None] * places[None, :] % modulus
    lowest = np.minimum(residue, modulus - residue)
    flipped = np.where(residue > modulus - residue, -1.0, 1.0).astype(np.float32)
    angle = lowest.astype(np.float32) * np.float32(2.0 * math.pi / modulus)
    sine = np.where(2 * lowest == modulus, np.float32(0.0), flipped * np.sin(angle))
    return np.cos(angle).astype(np.float32), sine.astype(np.float32)


def round_up(value, multiple):
    return -(-value // multiple) * multiple


@functools.lru_cache(maxsize=None)
def tables(width_rows, width_cols):
    half = width_cols // 2
    rows = width_rows // 2 + 1
    padded = round_up(rows, CHUNK)
    bf16 = ml_dtypes.bfloat16
    places = np.arange(width_cols)
    cos_v, sin_v = cos_sin(np.arange(half + 1), places, width_cols)
    packed_sin = sin_v[:half].copy()
    forward_sin = -packed_sin
    forward_sin[0] = cos_v[half]
    packed_sin[0] = cos_v[half]
    col = np.concatenate([cos_v[:half], forward_sin], 0).T.astype(bf16)
    back = (2.0 * np.concatenate([cos_v[:half], packed_sin], 0)[:, :OUTC].astype(bf16).astype(np.float32)).astype(bf16)
    cos_u, sin_u = cos_sin(np.arange(rows), np.arange(width_rows), width_rows)
    row = np.zeros((2 * padded, width_rows), np.float32)
    row[:rows] = cos_u
    row[padded : padded + rows] = -sin_u
    row = row.astype(bf16)
    weight = np.ones((rows, 1), np.float32)
    weight[0] = weight[-1] = 0.5
    out = np.zeros((2 * padded, STRIP), np.float32)
    out[:rows] = cos_u[:, :STRIP].astype(bf16).astype(np.float32) * weight
    out[padded : padded + rows] = sin_u[:, :STRIP].astype(bf16).astype(np.float32) * weight
    tall = round_up(padded, 128)
    out = np.concatenate([np.pad(part, ((0, tall - padded), (0, 0))) for part in (out[:padded], out[padded:])])
    out = np.ascontiguousarray(out.T).astype(bf16)
    row_sum = row[:, :TS].astype(np.float32).sum(1, keepdims=True)
    col_sum = col[:TS].astype(np.float32).sum(0, keepdims=True)
    return col, row, back, out, row_sum, col_sum


def swapped(value, axis, step):
    count = lax.axis_size(axis)
    return lax.ppermute(value, axis, [(source, source ^ step) for source in range(count)])


def spread_out(value, axis):
    held, step = {0: value}, lax.axis_size(axis) // 2
    while step > 1:
        held |= {index ^ step: swapped(block, axis, step) for index, block in held.items()}
        step //= 2
    return [held[index] for index in sorted(held)[1:]]


def with_partners(blocks, axis):
    return [block for held in blocks for block in (held, swapped(held, axis, 1))]


def dot(left, right):
    return jnp.dot(left, right, preferred_element_type=jnp.float32)


def tiles(padded, half, step):
    return [(slice(r, r + step), lane) for r in range(0, padded, step) for lane in range(0, half, LANES)]


def lanes(lane):
    return slice(lane, lane + LANES)


def where_first(lane, special, usual):
    if lane:
        return usual
    return jnp.where(lax.broadcasted_iota(jnp.int32, usual.shape, 1) == 0, special, usual)


def quadrants(load, rows, lane, padded, half):
    down = slice(padded + rows.start, padded + rows.stop)
    left, right = lanes(lane), lanes(half + lane)
    cc, cs, sc, ss = load(rows, left), load(rows, right), load(down, left), load(down, right)
    plus_re = cc - where_first(lane, 0.0, ss)
    plus_im = where_first(lane, 0.0, cs) + sc
    minus_re = where_first(lane, cs, cc + ss)
    minus_im = where_first(lane, ss, cs - sc)
    return plus_re, plus_im, minus_re, minus_im


def squared(signs):
    return signs[0] * signs[0] + signs[1] * signs[1], signs[2] * signs[2] + signs[3] * signs[3]


def sum_power(source_ref, power_ref, loads):
    padded, half = power_ref.shape[1:]
    total = 0.0
    for rows, lane in tiles(padded, half, STEP):
        at = lanes(lane)
        zero = jnp.zeros((STEP, LANES), jnp.float32)
        plus, minus = (zero, zero) if source_ref is None else (source_ref[0, rows, at], source_ref[1, rows, at])
        for load in loads:
            more = squared(quadrants(load, rows, lane, padded, half))
            plus, minus = plus + more[0], minus + more[1]
        power_ref[0, rows, at] = plus
        power_ref[1, rows, at] = minus
        total = total + (plus + minus)
    return total


def mean_power(total, power_ref, count, width_rows):
    last = width_rows // 2
    ends = [power_ref[0, r : r + 1] + power_ref[1, r : r + 1] for r in (0, last)]
    whole = 2.0 * jnp.sum(total, keepdims=True) - jnp.sum(ends[0] + ends[1], keepdims=True)
    return whole / (count * width_rows * 2 * power_ref.shape[2])


def whiten(power_ref, mean, count, ctf_ref, loads, weighted_ref):
    padded, half = power_ref.shape[1:]
    for rows, lane in tiles(padded, half, STEP):
        at = lanes(lane)
        gains = [lax.rsqrt(power_ref[side, rows, at] * (1.0 / count) + mean) for side in range(2)]
        for k, load in enumerate(loads):
            signs = quadrants(load, rows, lane, padded, half)
            for side in range(2):
                gain = gains[side] * ctf_ref[k, side, rows, at]
                weighted_ref[k, 2 * side, rows, at] = signs[2 * side] * gain
                weighted_ref[k, 2 * side + 1, rows, at] = signs[2 * side + 1] * gain


def ctf_kernel(half, width_rows, tile_ref, group_a, group_b, defocus_ref, ctf_ref):
    padded = ctf_ref.shape[2]
    shape_u, shape_v = (8, round_up(padded, 128)), (8, half)
    turns = []
    for k in range(2):
        group = jnp.where((tile_ref[0] & 1) == k, group_a[0], group_b[0])
        turns.append(jnp.float32(math.pi) * defocus_ref[group])

    def turn(shape):
        return jnp.where(lax.broadcasted_iota(jnp.int32, shape, 0) < 2, turns[0], turns[1])

    u = lax.broadcasted_iota(jnp.int32, shape_u, 1).astype(jnp.float32) / width_rows
    column = lax.broadcasted_iota(jnp.int32, shape_v, 1)
    wrapped = ((lax.broadcasted_iota(jnp.int32, shape_v, 0) & 1) == 1) & (column == 0)
    v = jnp.where(wrapped, half, column).astype(jnp.float32) / (2 * half)
    phase_u, phase_v = turn(shape_u) * (u * u) + 0.07, turn(shape_v) * (v * v)
    sin_u, cos_u = jnp.sin(phase_u).T, jnp.cos(phase_u).T
    sin_v, cos_v = jnp.sin(phase_v), jnp.cos(phase_v)
    for k in range(2):
        for r in range(0, padded, CHUNK):
            up, at = slice(r, r + CHUNK), slice(2 * k, 2 * k + 1)
            for side in range(2):
                row = slice(2 * k + side, 2 * k + side + 1)
                ctf_ref[k, side, up] = -(sin_u[up, at] * cos_v[row] + cos_u[up, at] * sin_v[row])


def pair_kernel(tile_ref, tpl_a, tpl_b, raw_ref, order_ref):
    bit, depth = tile_ref[0] & 1, tpl_a.shape[1]
    for index in range(raw_ref.shape[0]):
        for j, block in enumerate((tpl_a, tpl_b)):
            rows = pl.ds(pl.multiple_of((bit ^ j) * depth, depth), depth)
            order_ref[index, rows, :] = block[bit * raw_ref.shape[0] + index].astype(order_ref.dtype)
    raw_ref[...] = order_ref[...].astype(raw_ref.dtype)


def moments(block):
    wide = block.astype(jnp.float32)
    return jnp.sum(wide, axis=0, keepdims=True), jnp.sum(wide * wide, axis=0, keepdims=True)


def early_kernel(tile_ref, strip_a, strip_b, col_ref, row_ref, *outs):
    bit = tile_ref[0] & 1
    four = len(outs) == 3
    column_ref = outs[2] if four else outs[0]
    for j, strip in enumerate((strip_a, strip_b)):
        start = pl.multiple_of((bit ^ j) * STRIP, STRIP)
        column_ref[pl.ds(start, STRIP), :] = dot(strip[...], col_ref[...]).astype(jnp.bfloat16)
    if four:
        stage_kernel(0, tile_ref, column_ref, row_ref, *outs[:2])
    else:
        outs[1][0] = dot(row_ref[:, : 2 * STRIP], column_ref[...])
        outs[1][1] = dot(row_ref[:, :STRIP], column_ref[STRIP:, :])


def shape_kernel(tile_ref, raw_ref, col_ref, deep_ref, shape_ref, moment_ref):
    for index in range(shape_ref.shape[0]):
        for k, moment in enumerate(moments(raw_ref[index])):
            moment_ref[2 * index + k : 2 * index + k + 1, :] = moment
        columns = dot(raw_ref[index], col_ref[:TS, :]).astype(jnp.bfloat16)
        shape_ref[index] = dot(deep_ref[tile_ref[0] >> 1], columns)


def by_case(tile, body):
    def choose(low, high):
        if high - low == 1:
            return body(low)
        middle = (low + high) // 2
        lax.cond(tile < middle, lambda: choose(low, middle), lambda: choose(middle, high))

    choose(0, 4)


def rows_of(pair, offset, length):
    return pl.ds(pl.multiple_of(pair * (2 * STRIP), 2 * STRIP) + offset, length)


def other_kernel(count, tile_ref, *refs):
    others = refs[: count - 2]
    column_ref, col_ref, row_ref, part_ref, power_ref, work_ref = refs[count - 2 :]
    width_rows = row_ref.shape[1]
    tile = tile_ref[0]
    own, pairs = tile >> 1, count // 2
    for j in range(2, count):
        start = pl.multiple_of((tile ^ j) * STRIP, STRIP)
        part_ref[pl.ds(start, STRIP), :] = dot(others[j - 2][...], col_ref[...]).astype(jnp.bfloat16)
    part_ref[rows_of(own, 0, 2 * STRIP), :] = column_ref[...]
    for j in range(1, pairs):
        pair = own ^ j

        @pl.when(pair + 1 < pairs)
        def _():
            work_ref[0] = dot(row_ref[...], part_ref[rows_of(pair, 0, width_rows), :])
            work_ref[1] = dot(row_ref[...], part_ref[rows_of(pair, STRIP, width_rows), :])

        @pl.when(pair + 1 == pairs)
        def _():
            work_ref[0] = dot(row_ref[:, : 2 * STRIP], part_ref[rows_of(pair, 0, 2 * STRIP), :])
            work_ref[1] = dot(row_ref[:, :STRIP], part_ref[rows_of(pair, STRIP, STRIP), :])

        loads = [lambda rows, at, k=k: work_ref[k, rows, at] for k in range(2)]
        sum_power(None if j == 1 else power_ref, power_ref, loads)
    if pairs == 1:
        power_ref[...] = jnp.zeros(power_ref.shape, jnp.float32)


def own_kernel(count, tile_ref, part_ref, partial_ref, others_ref, ctf_ref, row_ref, weighted_ref, cross_ref, power_ref):
    width_rows = row_ref.shape[1]
    own, pairs = tile_ref[0] >> 1, count // 2

    def finish(loads):
        total = sum_power(others_ref, power_ref, loads)
        whiten(power_ref, mean_power(total, power_ref, count, width_rows), count, ctf_ref, loads, weighted_ref)

    @pl.when(own + 1 < pairs)
    def _():
        cross_ref[0] = dot(row_ref[:, 2 * STRIP :], part_ref[rows_of(own + 1, 0, width_rows - 2 * STRIP), :])
        cross_ref[1] = dot(row_ref[:, STRIP:], part_ref[rows_of(own + 1, 0, width_rows - STRIP), :])
        finish([lambda rows, at, k=k: partial_ref[k, rows, at] + cross_ref[k, rows, at] for k in range(2)])

    @pl.when(own + 1 == pairs)
    def _():
        finish([lambda rows, at, k=k: partial_ref[k, rows, at] for k in range(2)])


def span(strip, blocks):
    start = max(strip, blocks[0])
    stop = min((strip + 1) * STRIP + TS, (blocks[-1] + 1) * STRIP)
    return slice(start * STRIP - strip * STRIP, stop - strip * STRIP), slice(
        (start - blocks[0]) * STRIP, stop - blocks[0] * STRIP
    )


def reached(blocks):
    return [s for s in range(4) if s <= blocks[-1] and (s + 1) * STRIP + TS > blocks[0] * STRIP]


def sources(tile):
    sets = [[tile & 2, tile & 2 | 1], [tile ^ 2], [tile ^ 3]]
    strips = [reached(blocks) for blocks in sets]
    return sets, strips, [[k for k in range(3) if s in strips[k]] for s in range(4)]


def view(ref, strip):
    return lambda rows, at: ref[strip, rows, at]


def add_blocks(case, stage, block_ref, row_ref, quads):
    sets, strips, needs = sources(case)
    for s in strips[stage]:
        columns, rows = span(s, sets[stage])
        part = dot(row_ref[:, columns], block_ref[rows, :])
        before = [k for k in needs[s] if k < stage]
        quads[stage][s] = quads[before[-1]][s] + part if before else part


def stage_kernel(stage, tile_ref, *refs):
    earlier, refs = refs[:stage], refs[stage:]
    if stage:
        previous, strip_ref, col_ref, row_ref, quad_ref, power_ref, block_ref = refs
        block_ref[...] = dot(strip_ref[...], col_ref[...]).astype(jnp.bfloat16)
    else:
        previous, (block_ref, row_ref, quad_ref, power_ref) = None, refs
    quads = [*earlier, quad_ref]

    def body(case):
        add_blocks(case, stage, block_ref, row_ref, quads)
        needs = sources(case)[2]
        done = [s for s in range(4) if max(needs[s]) == stage]
        sum_power(previous, power_ref, [view(quads[needs[s][-1]], s) for s in done])

    by_case(tile_ref[0], body)


def last_kernel(
    tile_ref, first_ref, second_ref, previous_ref, strip_ref, col_ref, row_ref, ctf_ref,
    weighted_ref, third_ref, power_ref, block_ref,
):
    block_ref[...] = dot(strip_ref[...], col_ref[...]).astype(jnp.bfloat16)
    quads = [first_ref, second_ref, third_ref]

    def body(case):
        add_blocks(case, 2, block_ref, row_ref, quads)
        needs = sources(case)[2]
        loads = [view(quads[needs[s][-1]], s) for s in range(4)]
        total = sum_power(previous_ref, power_ref, [loads[s] for s in range(4) if max(needs[s]) == 2])
        mean = mean_power(total, power_ref, 4, STRIP + TS)
        whiten(power_ref, mean, 4, ctf_ref, loads[case & 2 : (case & 2) + 2], weighted_ref)

    by_case(tile_ref[0], body)


def score_kernel(count, tile_ref, *refs):
    pairs = count // 2
    others = refs[: pairs - 1]
    (weighted_ref, shape_ref, moment_ref, col_ref, deep_ref, back_ref, out_ref, row_sum_ref, col_sum_ref) = refs[
        pairs - 1 : pairs + 8
    ]
    score_ref, quad_ref, product_ref = refs[pairs + 8 :]
    padded, half = deep_ref.shape[1] // 2, col_ref.shape[1] // 2
    scale = 1.0 / ((STRIP + TS) * col_ref.shape[0])
    pieces, mine = score_ref.shape[:2]
    tile = tile_ref[0]
    tall = product_ref.shape[0] // 2
    for h in range(2):
        product_ref[tall * h + padded : tall * (h + 1), :] = jnp.zeros((tall - padded, 4 * half), jnp.bfloat16)
    for index in range(mine):
        sums, squares = (moment_ref[2 * index + k : 2 * index + k + 1, :] for k in range(2))
        for j in range(1, pairs):
            more = moments(others[j - 1][index])
            sums, squares = sums + more[0], squares + more[1]
            columns = dot(others[j - 1][index], col_ref[:TS, :]).astype(jnp.bfloat16)
            late = dot(deep_ref[(tile >> 1) ^ j], columns)
            quad_ref[...] = late if j == 1 else quad_ref[...] + late
        mean = jnp.sum(sums, keepdims=True) / (TS * TS)
        spread = jnp.sqrt(jnp.sum(squares, keepdims=True) / (TS * TS) - mean * mean + 1e-05)
        col_sum = mean * col_sum_ref[...]

        def load(rows, at):
            known = shape_ref[index, rows, at] + quad_ref[rows, at] if pairs > 1 else shape_ref[index, rows, at]
            return known - row_sum_ref[rows, :] * col_sum[:, at]

        for rows, lane in tiles(padded, half, CHUNK):
            a, b, c, d = quadrants(load, rows, lane, padded, half)
            for k in range(2):
                p, q, s, t = (weighted_ref[k, m, rows, lanes(lane)] for m in range(4))
                plus_re, plus_im = p * a + q * b, q * a - p * b
                minus_re, minus_im = s * c + t * d, t * c - s * d
                up, down = rows, slice(rows.start + tall, rows.stop + tall)
                left, right = lanes(2 * half * k + lane), lanes(2 * half * k + half + lane)
                parts = (
                    (up, left, plus_re + where_first(lane, 0.0, minus_re)),
                    (up, right, where_first(lane, minus_re, -(plus_im + minus_im))),
                    (down, left, where_first(lane, 0.0, minus_im) - plus_im),
                    (down, right, where_first(lane, -minus_im, minus_re - plus_re)),
                )
                for height, at, value in parts:
                    product_ref[height, at] = value.astype(jnp.bfloat16)
        for k in range(2):
            rows_first = dot(out_ref[...], product_ref[:, 2 * half * k : 2 * half * (k + 1)]).astype(jnp.bfloat16)
            score = dot(rows_first, back_ref[...]) * (scale / spread)
            strip = score.reshape(pieces // 2, 2 * STRIP // pieces, OUTC)
            score_ref[k * (pieces // 2) : (k + 1) * (pieces // 2), index] = strip.astype(jnp.bfloat16)


def on_device(kernel, scalars, operands, scratch, result, cost):
    vmem, smem = pl.BlockSpec(memory_space=pltpu.VMEM), pl.BlockSpec(memory_space=pltpu.SMEM)
    return pl.pallas_call(
        kernel,
        out_shape=result,
        in_specs=[smem] * len(scalars) + [vmem] * len(operands),
        out_specs=jax.tree.map(lambda _: vmem, result),
        scratch_shapes=scratch,
        compiler_params=pltpu.CompilerParams(vmem_limit_bytes=VMEM_BYTES),
        cost_estimate=None if cost is None else pl.CostEstimate(flops=cost, bytes_accessed=0, transcendentals=0),
    )(*scalars, *operands)


def local(micrograph, templates, defocus, group_of_tile):
    width_cols = micrograph.shape[1]
    width_rows = STRIP + TS
    tpl_count, depth = templates.shape[:2]
    count = lax.axis_size("tile")
    orient_count = lax.axis_size("orient")
    col, row, back, out, row_sum, col_sum = tables(width_rows, width_cols)
    deep = np.stack(np.split(row[:, :TS], count // 2, axis=1))
    padded, half = row.shape[0] // 2, width_cols // 2
    tile = lax.axis_index("tile").astype(jnp.int32).reshape(1)
    plane, quads = (padded, half), (2 * padded, width_cols)
    f32, bf16 = jnp.float32, jnp.bfloat16
    mine = tpl_count // 2
    pass_flops = 2 * quads[0] * quads[1] * STRIP

    strips = spread_out(micrograph, "tile")
    raw = on_device(
        pair_kernel,
        [tile],
        [templates, swapped(templates, "tile", 1)],
        [pltpu.VMEM((mine, 2 * depth, TS), bf16 if depth % 16 == 0 else f32)],
        jax.ShapeDtypeStruct((mine, 2 * depth, TS), bf16),
        None,
    )
    ctf = on_device(
        functools.partial(ctf_kernel, half, width_rows),
        [tile, group_of_tile, swapped(group_of_tile, "tile", 1), defocus],
        [],
        [],
        jax.ShapeDtypeStruct((2, 2, *plane), f32),
        20 * pass_flops,
    )
    early_in = [micrograph, swapped(micrograph, "tile", 1), col, row]
    shape_out = (
        jax.ShapeDtypeStruct((mine, *quads), f32),
        jax.ShapeDtypeStruct((round_up(2 * mine, 8), TS), f32),
    )
    columns_out = jax.ShapeDtypeStruct((2 * STRIP, width_cols), bf16)
    all_quads, power_out = jax.ShapeDtypeStruct((4, *quads), f32), jax.ShapeDtypeStruct((2, *plane), f32)
    weighted_out = jax.ShapeDtypeStruct((2, 4, *plane), f32)
    if count == 4:
        shape, moment = on_device(shape_kernel, [tile], [raw, col, deep], [], shape_out, None)
        early_in[0], shape = lax.optimization_barrier((early_in[0], shape))
        pieces = spread_out(raw, "tile")
        quads_0, power = on_device(
            early_kernel,
            [tile],
            early_in,
            [pltpu.VMEM(columns_out.shape, bf16)],
            (all_quads, power_out),
            None,
        )
        strips, power, ctf, shape = lax.optimization_barrier((strips, power, ctf, shape))
        block = pltpu.VMEM((STRIP, width_cols), bf16)
        quads_1, power = on_device(
            functools.partial(stage_kernel, 1),
            [tile],
            [quads_0, power, strips[0], col, row],
            [block],
            (all_quads, power_out),
            30 * pass_flops,
        )
        weighted = on_device(
            last_kernel,
            [tile],
            [quads_0, quads_1, power, swapped(strips[0], "tile", 1), col, row, ctf],
            [pltpu.VMEM((4, *quads), f32), pltpu.VMEM((2, *plane), f32), block],
            weighted_out,
            12 * pass_flops,
        )
    else:
        column, partial = on_device(
            early_kernel,
            [tile],
            early_in,
            [],
            (columns_out, jax.ShapeDtypeStruct((2, *quads), f32)),
            None,
        )
        pieces = spread_out(raw, "tile")
        shape, moment = on_device(shape_kernel, [tile], [raw, col, deep], [], shape_out, None)
        strips, column, ctf = lax.optimization_barrier((strips, column, ctf))
        part, power = on_device(
            functools.partial(other_kernel, count),
            [tile],
            [*with_partners(strips, "tile"), column, col, row],
            [pltpu.VMEM((2, *quads), f32)],
            (jax.ShapeDtypeStruct((count * STRIP, width_cols), bf16), power_out),
            None,
        )
        weighted = on_device(
            functools.partial(own_kernel, count),
            [tile],
            [part, partial, power, ctf, row],
            [pltpu.VMEM((2, *quads), f32), pltpu.VMEM((2, *plane), f32)],
            weighted_out,
            None,
        )
    scores = on_device(
        functools.partial(score_kernel, count),
        [tile],
        [*pieces, weighted, shape, moment, col, deep, back, out, row_sum, col_sum],
        [
            pltpu.VMEM(quads, f32),
            pltpu.VMEM((out.shape[1], 2 * width_cols), bf16),
        ],
        jax.ShapeDtypeStruct((2 * orient_count, mine, STRIP // orient_count, OUTC), bf16),
        None,
    )
    chips = [[first + k for k in range(2 * orient_count)] for first in range(0, count * orient_count, 2 * orient_count)]
    received = lax.all_to_all(
        scores, ("tile", "orient"), split_axis=0, concat_axis=0, tiled=True, axis_index_groups=chips
    ).astype(f32)
    orient_total = tpl_count * orient_count
    best = jnp.max(received, axis=(0, 1))
    score_mean = jnp.sum(received, axis=(0, 1)) / orient_total
    score_var = jnp.sum(received * received, axis=(0, 1)) / orient_total - score_mean * score_mean
    return (best, (best - score_mean) / jnp.sqrt(score_var + 1e-05))


def solution(mesh):
    placed = (P("tile", None), P("orient", "tile", None), P(), P("tile"))
    return jax.shard_map(
        local,
        mesh=mesh,
        in_specs=placed,
        out_specs=(P(("tile", "orient"), None), P(("tile", "orient"), None)),
        check_vma=False,
    )
```
